256 devices in a mesh: dp: 32 (over z, y), tensor: 8 (over x, core).
Axes of the slice: x: 4, y: 4, z: 8, core: 2. Of those that a mesh axis runs over, the one named last changes fastest.
Arguments:
- queries: bfloat16 [24576, 4096], P('dp', 'tensor'), may hold values from -8 to 8
- step_kv: bfloat16 [2, 24576, 1024], P(None, 'dp', 'tensor'), may hold values from -6 to 6
- tile_kv: bfloat16 [2, 262144, 1024], P(None, 'dp', 'tensor'), may hold values from -6 to 6
- tile_slot: int32 [1024], replicated, may hold values from 0 to 127, as said below
- step_lengths: int32 [128, 8], replicated, may hold values from 1 to 24, 120 in all within a row
- parents: int32 [128, 8], replicated, may hold values from -1 to 6, as said below
- out_weight: bfloat16 [4096, 8192], P('dp', 'tensor'), may hold values from -0.09375 to 0.09375
Outputs:
- mixed_out: bfloat16 [24576, 8192], P('dp', 'tensor')
The draws below stay inside these ranges and needn't reach their ends.
Inputs may be any that keep to these rules, and one draw needn't show every extreme that they name: `tile_slot`: tile t is encoded on index t // 32 of dp; problem p's steps lie on index p // 4 of dp. Each problem owns 1 to 12 tiles and on every index one of its problems owns exactly 12; the problems of one index own exactly 32 tiles together; the tiles of one encoding index that belong to the problems of one index number at most 2, and exactly 2 for some. parents[p, 0] = -1; for s >= 1, parents[p, s] is a step before s. `step_lengths`: row p holds the token counts of problem p's 8 steps.
All inputs are finite; a program needn't handle non-finite values.
Results may differ from the reference program's by a relative error of at most 0.0052.
Values may be sent and summed in bfloat16 or wider, within the bound.
A program may use at most 128 MiB of HBM per device.

```python
import math
import jax
import jax.numpy as jnp
import numpy as np
from jax import lax

D = 8192
HQ = 32
KVH = 8
HD = 128
TILE = 256
TILE_MAX = 12
STEPS = 8
STEP_LEN = 24
PROB_DEV = 4
TILE_DEV = 32
CAP = 2
PROBS = 128
TILES = 1024
TOKENS = 24576


def draw_queries(key, part):
    key = jax.random.fold_in(key, 1)
    group_size = HQ // KVH
    drawn = jnp.clip(2.2 * jax.random.normal(key, (TOKENS, KVH, group_size, HD), jnp.float32), -8.0, 8.0)
    return drawn.reshape(TOKENS, HQ * HD).astype(jnp.bfloat16)


def draw_step_kv(key, part):
    key = jax.random.fold_in(key, 2)
    key_part, value_part = jax.random.split(key)
    key_rows = jnp.clip(1.3 * jax.random.normal(key_part, (TOKENS, KVH, HD), jnp.float32), -6.0, 6.0)
    value_rows = jnp.clip(jax.random.normal(value_part, (TOKENS, KVH * HD), jnp.float32), -5.0, 5.0)
    return jnp.stack([key_rows.reshape(TOKENS, KVH * HD), value_rows]).astype(jnp.bfloat16)


def draw_tile_slot(key, part):
    key = jax.random.fold_in(key, 7)
    key_list = jax.random.split(key, 5)
    senders = TILES // TILE_DEV
    shift_pool = jnp.arange(senders * CAP, dtype=jnp.int32) // CAP
    first_shift = jax.random.randint(key_list[0], (), 0, senders)
    shuffled = jax.random.permutation(key_list[1], senders * CAP).astype(jnp.int32)
    ranking = jnp.where(shift_pool == first_shift, jnp.arange(senders * CAP, dtype=jnp.int32), senders * CAP + shuffled)
    shifts = shift_pool[jnp.argsort(ranking)][:TILE_DEV]
    relabel = jax.random.permutation(key_list[2], senders).astype(jnp.int32)
    tile_index = jnp.arange(TILES, dtype=jnp.int32)
    encoder = tile_index // TILE_DEV
    destination = relabel[(encoder + shifts[tile_index % TILE_DEV]) % senders]
    matches = (destination[:, None] == jnp.arange(senders, dtype=jnp.int32)[None, :]).astype(jnp.int32)
    arrival = jnp.sum((jnp.cumsum(matches, axis=0) - 1) * matches, axis=1)
    forced = jax.random.randint(key_list[3], (senders,), 0, PROB_DEV)
    slot_ids = jnp.arange(PROB_DEV, dtype=jnp.int32)
    counts = jnp.where(slot_ids[None, :] == forced[:, None], TILE_MAX, 1).astype(jnp.int32)

    def add_one(step_number, counts):
        probe_start = jax.random.randint(jax.random.fold_in(key_list[4], step_number), (senders,), 0, PROB_DEV)
        open_slots = counts < TILE_MAX
        distance = (slot_ids[None, :] - probe_start[:, None]) % PROB_DEV
        picked = jnp.argmin(jnp.where(open_slots, distance, PROB_DEV), axis=1).astype(jnp.int32)
        return counts + (slot_ids[None, :] == picked[:, None]).astype(jnp.int32)
    counts = lax.fori_loop(0, TILE_DEV - TILE_MAX - PROB_DEV + 1, add_one, counts)
    slot_ends = jnp.cumsum(counts, axis=1)
    slot_number = jnp.sum((arrival[:, None] >= slot_ends[destination]).astype(jnp.int32), axis=1)
    return (destination * PROB_DEV + slot_number).astype(jnp.int32)


def draw_parents(key, part):
    key = jax.random.fold_in(key, 5)
    first_key, second_key = jax.random.split(key)
    column = jnp.arange(STEPS, dtype=jnp.int32)[None, :]
    upper = jnp.broadcast_to(jnp.maximum(column, 1), (PROBS, STEPS))
    drawn = jax.random.randint(first_key, (PROBS, STEPS), 0, upper)
    chosen_row = jax.random.randint(second_key, (), 0, PROBS)
    row_index = jnp.arange(PROBS, dtype=jnp.int32)[:, None]
    drawn = jnp.where((row_index == chosen_row) & (column == STEPS - 1), STEPS - 2, drawn)
    return jnp.where(column == 0, -1, drawn).astype(jnp.int32)


def shard_levels(own_key, dims, cuts, least, top_value):
    def one(dim, shards_of):
        heights = jax.random.uniform(jax.random.fold_in(jax.random.fold_in(own_key, 6), dim), (shards_of,), jnp.float32, least / len(cuts), top_value / len(cuts))
        return jnp.repeat(jnp.exp(heights), dims[dim] // shards_of).reshape((-1,) + (1,) * (len(dims) - dim - 1))

    gain = one(*cuts[0])
    for cut in cuts[1:]:
        gain = gain * one(*cut)
    return gain


def length_profile(count, total, bound, lean):
    weights = [(1 << 20) // math.isqrt(grade ** lean) + 1 for grade in range(2, count + 1)]
    rest, given = total - bound - (count - 1), [1] * (count - 1)
    while rest > 0:
        free = [i for i in range(count - 1) if given[i] < bound]
        whole, budget = sum([weights[i] for i in free]), rest
        for i in free:
            more = min(bound - given[i], max(1, budget * weights[i] // whole), rest)
            given[i] = given[i] + more
            rest = rest - more
    return np.array([bound] + given)


def ragged_sizes(key, count, total, limit, lean):
    if count == 2:
        one = jax.random.randint(key, (), max(1, total - limit), min(limit, total - 1) + 1)
        return jnp.stack([one, total - one])
    lengths = jnp.asarray(length_profile(count, total, limit, lean), jnp.int32)
    pairs = (count - 1) // 2
    giver, receiver = lengths[1:1 + 2 * pairs:2], lengths[2:2 + 2 * pairs:2]
    margin = jnp.minimum(giver - 1, limit - receiver)
    moved = jax.random.randint(jax.random.fold_in(key, 1), (pairs,), 0, 1 << 20) % (margin + 1)
    lengths = lengths.at[1:1 + 2 * pairs:2].set(giver - moved).at[2:2 + 2 * pairs:2].set(receiver + moved)
    return lengths[jax.random.permutation(jax.random.fold_in(key, 2), count)]


def normal_values(stream_key, extent, scale, most, pieces=(), kind=jnp.bfloat16):
    factor_of = shard_levels(stream_key, extent, pieces, -0.22, 0.18) if pieces else 1.0
    values = jax.random.normal(stream_key, extent, jnp.float32) * scale * factor_of
    return jnp.minimum(jnp.maximum(values, -most), most).astype(kind)


def setup_inputs(seed: int = 0) -> dict:
    seeds = jax.random.split(jax.random.key(seed), 8)
    queries = draw_queries(jax.random.fold_in(seeds[7], 71), 0)
    step_kv = draw_step_kv(jax.random.fold_in(seeds[7], 71), 0)
    tile_kv = normal_values(seeds[2], (2, TILES * TILE, KVH * HD), 1.3, 6.0, ((1, 32), (2, 8)))
    tile_slot = draw_tile_slot(jax.random.fold_in(seeds[7], 71), 0)
    step_lengths = jax.vmap(lambda own: ragged_sizes(own, STEPS, STEPS * STEP_LEN * 5 // 8, STEP_LEN, 1))(jax.random.split(seeds[4], PROBS)).reshape((PROBS, STEPS)).astype(jnp.int32)
    parents = draw_parents(jax.random.fold_in(seeds[7], 71), 0)
    out_weight = normal_values(seeds[6], (HQ * HD, D), (HQ * HD) ** -0.5, 0.09375, ((0, 32), (1, 8)))
    return {"queries": queries, "step_kv": step_kv, "tile_kv": tile_kv, "tile_slot": tile_slot, "step_lengths": step_lengths, "parents": parents, "out_weight": out_weight}


def ancestry(parents_row):
    parent_links = (parents_row[:, None] == jnp.arange(STEPS, dtype=jnp.int32)[None, :]).astype(jnp.int32)
    reached = jnp.eye(STEPS, dtype=jnp.int32)
    frontier = reached
    for depth_step in range(STEPS - 1):
        frontier = jnp.minimum(jnp.dot(frontier, parent_links), 1)
        reached = jnp.maximum(reached, frontier)
    return reached > 0

def visibility(lengths_row, parents_row):
    reached = ancestry(parents_row)
    token_index = jnp.arange(STEPS * STEP_LEN, dtype=jnp.int32)
    step_of = token_index // STEP_LEN
    position = token_index % STEP_LEN
    reached_full = jnp.repeat(jnp.repeat(reached, STEP_LEN, axis=0), STEP_LEN, axis=1)
    length_of = jnp.repeat(lengths_row, STEP_LEN)
    key_live = position < length_of
    same_step = step_of[:, None] == step_of[None, :]
    visible = reached_full & key_live[None, :] & (jnp.logical_not(same_step) | (position[None, :] <= position[:, None]))
    return (visible, key_live)

def attend(query_block, key_rows, value_rows, key_mask, live_rows):
    scores = jnp.einsum('qkgd,nkd->kgqn', query_block.astype(jnp.float32), key_rows.astype(jnp.float32)) / math.sqrt(HD)
    scores = jnp.where(key_mask[None, None], scores, -jnp.inf)
    row_max = lax.optimization_barrier(jnp.max(scores, axis=-1, keepdims=True))
    exponent = jnp.exp(scores - row_max)
    totals = lax.optimization_barrier(jnp.sum(exponent, axis=-1, keepdims=True))
    weights = exponent.astype(jnp.bfloat16)
    result = jnp.einsum('kgqn,nkd->qkgd', weights.astype(jnp.float32), value_rows.astype(jnp.float32))
    result = result / jnp.transpose(totals, (2, 0, 1, 3))
    result = jnp.where(live_rows[:, None, None, None], result, 0.0)
    return result.astype(jnp.bfloat16)

def reference(queries, step_kv, tile_kv, tile_slot, step_lengths, parents, out_weight):
    step_span = STEPS * STEP_LEN
    group_size = HQ // KVH
    tile_array = tile_kv.reshape(2, TILES, TILE, KVH, HD)
    query_all = queries.reshape(PROBS, step_span, KVH, group_size, HD)
    step_all = step_kv.reshape(2, PROBS, step_span, KVH, HD)

    def per_problem(problem):
        owned = tile_slot == problem
        picked = jnp.nonzero(owned, size=TILE_MAX, fill_value=0)[0].astype(jnp.int32)
        tile_total = jnp.sum(owned.astype(jnp.int32))
        tile_live = jnp.arange(TILE_MAX, dtype=jnp.int32) < tile_total
        chosen = jnp.take(tile_array, picked, axis=1).reshape(2, TILE_MAX * TILE, KVH, HD)
        step_here = lax.dynamic_index_in_dim(step_all, problem, 1, keepdims=False)
        key_rows = jnp.concatenate([chosen[0], step_here[0]], axis=0)
        value_rows = jnp.concatenate([chosen[1], step_here[1]], axis=0)
        visible, live_rows = visibility(step_lengths[problem], parents[problem])
        tile_seen = jnp.broadcast_to(jnp.repeat(tile_live, TILE)[None, :], (step_span, TILE_MAX * TILE))
        key_mask = jnp.concatenate([tile_seen, visible], axis=1)
        query_block = lax.dynamic_index_in_dim(query_all, problem, 0, keepdims=False)
        head_out = attend(query_block, key_rows, value_rows, key_mask, live_rows).reshape(step_span, HQ * HD)
        return jnp.dot(head_out, out_weight, preferred_element_type=jnp.float32).astype(jnp.bfloat16)
    mixed_out = lax.map(per_problem, jnp.arange(PROBS, dtype=jnp.int32))
    return mixed_out.reshape(TOKENS, D)
```

```python
import functools
import math

import jax
import jax.numpy as jnp
from jax import lax
from jax.experimental import pallas as pl
from jax.experimental.pallas import tpu as pltpu
from jax.sharding import PartitionSpec as P

HD = 128
TILE = 256
STEPS = 8
STEP_LEN = 24
SPAN = STEPS * STEP_LEN
PROBLEMS = 4
GROUP = 4
LIVE = 128
LANES = GROUP * LIVE
Z = 8
Y = 4
X = 4
LOW = -1e30
SCALE = math.log2(math.e) / math.sqrt(HD)
MESH = pl.DeviceIdType.MESH
ORDER = (4, 3, 5, 2, 6, 1, 7, 0)
MIB = 1 << 20

META_ORDER = 0
META_OWNER = 64
META_SAME = 128
META_LAST = 192


def dot(a, b, dims=((1,), (0,))):
    return lax.dot_general(a, b, (dims, ((), ())), preferred_element_type=jnp.float32)


def prep_kernel(
    slot_ref, length_ref, parent_ref, query_ref, tile_ref,
    send_ref, qt_ref, mask_ref, expand_ref, meta_ref,
    count, count_in, owner_of, sems,
):
    dp = lax.axis_index("dp")
    z, y = dp // Y, dp % Y

    def clear(i, _):
        count[i] = 0
        count_in[i] = 0
        return 0

    lax.fori_loop(0, 32, clear, 0)

    def clear_slots(i, _):
        owner_of[i] = -1
        meta_ref[META_ORDER + i] = 0
        meta_ref[META_OWNER + i] = 0
        meta_ref[META_SAME + i] = 0
        meta_ref[META_LAST + i] = 0
        return 0

    lax.fori_loop(0, 64, clear_slots, 0)

    def place(t, _):
        d = slot_ref[dp * 32 + t] >> 2
        rz = ((d >> 2) - z) & 7
        r = ((d & 3) - y) & 3
        j = count[r * 8 + rz]
        count[r * 8 + rz] = j + 1
        pltpu.make_async_copy(
            tile_ref.at[:, pl.ds(pl.multiple_of(t * TILE, TILE), TILE), :],
            send_ref.at[r, rz, j],
            sems.at[t],
        ).start()
        return 0

    lax.fori_loop(0, 32, place, 0)

    def arrive(q, _):
        s = slot_ref[z * 128 + q]
        d = s >> 2

        @pl.when((d & 3) == y)
        def _():
            rz = ((d >> 2) - z) & 7
            r = (y - (q >> 5)) & 3
            j = count_in[r * 8 + rz]
            count_in[r * 8 + rz] = j + 1
            owner_of[rz * 8 + r * 2 + j] = s & 3

        return 0

    lax.fori_loop(0, 128, arrive, 0)

    def arrange(i, n):
        rz, p = i // 4, i % 4
        n = jnp.where(p == 0, 0, n)

        def scan(s, carry):
            n, seen = carry
            match = owner_of[rz * 8 + s] == p

            @pl.when(match)
            def _():
                meta_ref[META_ORDER + rz * 8 + n] = s
                meta_ref[META_OWNER + rz * 8 + n] = p
                meta_ref[META_SAME + rz * 8 + n] = seen
                meta_ref[META_LAST + rz * 4 + p] = n + 1

            hit = match.astype(jnp.int32)
            return n + hit, jnp.maximum(seen, hit)

        n, _ = lax.fori_loop(0, 8, scan, (n, 0))
        return n

    lax.fori_loop(0, 32, arrange, 0)

    row = lax.broadcasted_iota(jnp.int32, (SPAN, LIVE), 0)
    lane = lax.broadcasted_iota(jnp.int32, (SPAN, LIVE), 1)
    step_of = row // STEP_LEN
    position = row - step_of * STEP_LEN
    for p in range(PROBLEMS):
        problem = dp * PROBLEMS + p
        lengths = [length_ref[problem, s] for s in range(STEPS)]
        links = [parent_ref[problem, s] for s in range(STEPS)]
        starts, lines = [], []
        total = jnp.int32(0)
        for s in range(STEPS):
            starts.append(total)
            total = total + lengths[s]
            line = jnp.int32(1 << s)
            for b in range(s):
                line = line | jnp.where(links[s] == b, lines[b], 0)
            lines.append(line)
        row_start, row_length = jnp.zeros_like(row), jnp.zeros_like(row)
        row_bit = jnp.zeros_like(row)
        lane_step, lane_start, lane_line = jnp.zeros_like(row), jnp.zeros_like(row), jnp.zeros_like(row)
        for s in range(STEPS):
            here = step_of == s
            row_start = jnp.where(here, starts[s], row_start)
            row_length = jnp.where(here, lengths[s], row_length)
            row_bit = jnp.where(here, 1 << s, row_bit)
            passed = lane >= starts[s]
            lane_step = jnp.where(passed, s, lane_step)
            lane_start = jnp.where(passed, starts[s], lane_start)
            lane_line = jnp.where(passed, lines[s], lane_line)
        live = position < row_length
        picked = (lane == row_start + position) & live
        expand = jnp.where(picked, 1.0, 0.0).astype(jnp.bfloat16)
        expand_ref[p] = expand
        visible = (
            ((lane_line & row_bit) != 0)
            & live
            & ((step_of != lane_step) | (position <= lane - lane_start))
        )
        mask_ref[p] = jnp.where(visible, 1.0, 0.0)
        for h in range(GROUP):
            block = query_ref[p * SPAN : (p + 1) * SPAN, h * HD : (h + 1) * HD]
            qt_ref[p, :, h * LIVE : (h + 1) * LIVE] = dot(block, expand, ((0,), (0,))).astype(
                jnp.bfloat16
            )

    def settle(t, _):
        pltpu.make_async_copy(
            tile_ref.at[:, pl.ds(0, TILE), :], send_ref.at[0, 0, 0], sems.at[t]
        ).wait()
        return 0

    lax.fori_loop(0, 32, settle, 0)


def plane_kernel(
    meta_ref, send_ref, qt_ref, step_ref, mask_ref,
    out_ref,
    *scratch,
):
    tiles = scratch[0:8]
    qs = (qt_ref,) + tuple(scratch[8:15])
    (
        relay, state_o, state_m, state_l, step_o, step_m, step_l,
        up_in, up_in_s, up_out, up_out_s, down_in, down_in_s, down_out, down_out_s,
        own_sem, y_send, y_recv, q_send, q_recv, c_send, c_recv, x_send, x_recv,
    ) = scratch[15:]
    dp, tensor = lax.axis_index("dp"), lax.axis_index("tensor")
    z, y = dp // Y, dp % Y
    x, core = tensor // 2, tensor % 2
    y_up = (z * Y + (y + 1) % Y, tensor)
    y_down = (z * Y + (y + Y - 1) % Y, tensor)
    z_up = (((z + 1) % Z) * Y + y, tensor)
    z_down = (((z + Z - 1) % Z) * Y + y, tensor)
    x_up = (dp, ((x + 1) % X) * 2 + core)
    x_down = (dp, ((x + X - 1) % X) * 2 + core)
    mate = (dp, x * 2 + 1 - core)

    barrier = pltpu.get_barrier_semaphore()
    peers = (y_up, y_down, z_up, z_down, x_up, x_down, mate)
    for peer in peers:
        pl.semaphore_signal(barrier, inc=1, device_id=peer, device_id_type=MESH)
    pl.semaphore_wait(barrier, len(peers))

    def remote(src, dst, send_sem, recv_sem, peer):
        return pltpu.make_async_remote_copy(
            src_ref=src, dst_ref=dst, send_sem=send_sem, recv_sem=recv_sem,
            device_id=peer, device_id_type=MESH,
        )

    def q_copies(hop):
        up_from, up_to = (8 - hop) % 8, 7 - hop
        up_src, up_dst = qs[up_from], qs[up_to]
        down_src, down_dst = qs[hop], qs[hop + 1]
        if hop == 3:
            up_src, up_dst = up_src.at[pl.ds(0, 2)], up_dst.at[pl.ds(0, 2)]
            down_src, down_dst = down_src.at[pl.ds(2, 2)], down_dst.at[pl.ds(2, 2)]
        return (
            remote(up_src, up_dst, q_send.at[hop, 0], q_recv.at[hop, 0], z_up),
            remote(down_src, down_dst, q_send.at[hop, 1], q_recv.at[hop, 1], z_down),
        )

    def direct(i):
        rz = ORDER[i]
        return (
            remote(send_ref.at[1, rz], tiles[rz].at[pl.ds(2, 2)], y_send.at[i, 0], y_recv.at[i, 0], y_up),
            remote(send_ref.at[3, rz], tiles[rz].at[pl.ds(6, 2)], y_send.at[i, 1], y_recv.at[i, 1], y_down),
        )

    def first_leg(i):
        rz = ORDER[i]
        return (
            remote(send_ref.at[2, rz, 0], relay.at[i, 0], y_send.at[i, 2], y_recv.at[i, 2], y_up),
            remote(send_ref.at[2, rz, 1], relay.at[i, 1], y_send.at[i, 3], y_recv.at[i, 3], y_down),
        )

    def second_leg(i):
        rz = ORDER[i]
        return (
            remote(relay.at[i, 0], tiles[rz].at[4], y_send.at[i, 4], y_recv.at[i, 4], y_up),
            remote(relay.at[i, 1], tiles[rz].at[5], y_send.at[i, 5], y_recv.at[i, 5], y_down),
        )

    def own(i):
        rz = ORDER[i]
        return pltpu.make_async_copy(send_ref.at[0, rz], tiles[rz].at[pl.ds(0, 2)], own_sem.at[i])

    def start(copies):
        for copy in copies:
            copy.start()

    def arrived(copies):
        for copy in copies:
            copy.wait_recv()

    def pass_on(i):
        arrived(first_leg(i))
        start(second_leg(i))

    start(q_copies(0))
    for i in range(4):
        start(first_leg(i))
        if i < 3:
            start(direct(i))
    for i in range(8):
        own(i).start()

    state_o[0] = jnp.zeros((HD, LANES), jnp.float32)
    state_m[0] = jnp.full((1, LANES), LOW, jnp.float32)
    state_l[0] = jnp.zeros((1, LANES), jnp.float32)

    def soften(scores, m_before):
        m = jnp.maximum(m_before, jnp.max(scores, axis=0, keepdims=True))
        expo = jnp.exp2(scores - m)
        return m, jnp.sum(expo, axis=0, keepdims=True), expo.astype(jnp.bfloat16)

    def attend_steps(p, _):
        rows = pl.ds(pl.multiple_of(p * SPAN, SPAN), SPAN)
        mask = mask_ref[p]
        mask = jnp.concatenate([mask] * GROUP, axis=1)
        scores = dot(step_ref[0, rows, :], qt_ref[p]) * SCALE
        scores = jnp.where(mask > 0.5, scores, LOW)
        m, l, weights = soften(scores, jnp.full((1, LANES), LOW, jnp.float32))
        step_o[p] = dot(step_ref[1, rows, :], weights, ((0,), (0,)))
        step_m[p] = m
        step_l[p] = l
        return 0

    def attend_tiles(rz):
        def one(s, _):
            slot = meta_ref[META_ORDER + rz * 8 + s]
            owner = meta_ref[META_OWNER + rz * 8 + s]
            same = meta_ref[META_SAME + rz * 8 + s]
            scores = dot(tiles[rz][slot, 0], qs[rz][owner]) * SCALE
            m_before = jnp.where(same > 0, state_m[s], LOW)
            m, l, weights = soften(scores, m_before)
            alpha = jnp.exp2(m_before - m)
            state_o[s + 1] = state_o[s] * alpha + dot(tiles[rz][slot, 1], weights, ((0,), (0,)))
            state_m[s + 1] = m
            state_l[s + 1] = state_l[s] * alpha + l
            return 0

        lax.fori_loop(0, 8, one, 0)

    def chain_copies(hop, out, out_s, inn, inn_s, side, peer):
        src, dst = out.at[hop], inn.at[hop]
        if hop == 0:
            half = pl.ds(2, 2) if side == 0 else pl.ds(0, 2)
            src, dst = out.at[hop, half], inn.at[hop, half]
        return (
            remote(src, dst, c_send.at[hop, side, 0], c_recv.at[hop, side, 0], peer),
            remote(out_s.at[hop], inn_s.at[hop], c_send.at[hop, side, 1], c_recv.at[hop, side, 1], peer),
        )

    def up(hop):
        return chain_copies(hop, up_out, up_out_s, up_in, up_in_s, 0, z_up)

    def down(hop):
        return chain_copies(hop, down_out, down_out_s, down_in, down_in_s, 1, z_down)

    def pass_sums(hop, rz, side):
        copies = (up, down)[side]
        out, out_s, inn, inn_s = (
            (up_out, up_out_s, up_in, up_in_s),
            (down_out, down_out_s, down_in, down_in_s),
        )[side]
        if hop > 0:
            arrived(copies(hop - 1))
        else:
            out_s[hop] = jnp.zeros((8, LANES), jnp.float32)

        def alone(p, _):
            last = meta_ref[META_LAST + rz * 4 + p]
            out[hop, p] = state_o[last].astype(jnp.bfloat16)
            out_s[hop, pl.ds(p, 1), :] = state_m[last]
            out_s[hop, pl.ds(p + 4, 1), :] = state_l[last]
            return 0

        def merged(p, _):
            last = meta_ref[META_LAST + rz * 4 + p]
            m_a, m_b = state_m[last], inn_s[hop - 1, pl.ds(p, 1), :]
            m = jnp.maximum(m_a, m_b)
            a, b = jnp.exp2(m_a - m), jnp.exp2(m_b - m)
            out[hop, p] = (state_o[last] * a + inn[hop - 1, p].astype(jnp.float32) * b).astype(
                jnp.bfloat16
            )
            out_s[hop, pl.ds(p, 1), :] = m
            out_s[hop, pl.ds(p + 4, 1), :] = (
                state_l[last] * a + inn_s[hop - 1, pl.ds(p + 4, 1), :] * b
            )
            return 0

        half = (2, 4) if side == 0 else (0, 2)
        other = (0, 2) if side == 0 else (2, 4)
        if hop == 0:
            lax.fori_loop(*half, alone, 0)
        elif hop == 1:
            lax.fori_loop(*half, merged, 0)
            lax.fori_loop(*other, alone, 0)
        else:
            lax.fori_loop(0, 4, merged, 0)
        start(copies(hop))

    for hop in range(3):
        arrived(q_copies(hop))
        start(q_copies(hop + 1))
        pass_on(hop)
    lax.fori_loop(0, PROBLEMS, attend_steps, 0)

    for i in range(8):
        rz = ORDER[i]
        arrived(direct(i))
        arrived(second_leg(i))
        own(i).wait()
        if i + 3 < 8:
            start(direct(i + 3))
            if i + 4 < 8:
                start(first_leg(i + 4))
            pass_on(i + 3)
        if i == 0:
            arrived(q_copies(3))
        attend_tiles(rz)
        if rz == 4:
            pass_sums(0, rz, 0)
            pass_sums(0, rz, 1)
        elif rz in (3, 2, 1):
            pass_sums(4 - rz, rz, 0)
        elif rz in (5, 6, 7):
            pass_sums(rz - 4, rz, 1)
    arrived(up(3))
    arrived(down(3))

    mine = tensor

    def finish(p, _):
        last = meta_ref[META_LAST + p]
        terms = (
            (state_o[last], state_m[last], state_l[last]),
            (step_o[p], step_m[p], step_l[p]),
            (up_in[3, p].astype(jnp.float32), up_in_s[3, pl.ds(p, 1), :], up_in_s[3, pl.ds(p + 4, 1), :]),
            (down_in[3, p].astype(jnp.float32), down_in_s[3, pl.ds(p, 1), :], down_in_s[3, pl.ds(p + 4, 1), :]),
        )
        m = functools.reduce(jnp.maximum, [t[1] for t in terms])
        factors = [jnp.exp2(t[1] - m) for t in terms]
        total = sum(t[2] * f for t, f in zip(terms, factors))
        result = sum(t[0] * f for t, f in zip(terms, factors)) / total
        rows = pl.ds(pl.multiple_of(p * LIVE, LIVE), LIVE)
        for h in range(GROUP):
            block = result[:, h * LIVE : (h + 1) * LIVE]
            out_ref[mine, rows, h * HD : (h + 1) * HD] = block.T.astype(jnp.bfloat16)
        return 0

    lax.fori_loop(0, PROBLEMS, finish, 0)

    ROWS = PROBLEMS * LIVE
    left = ((x + X - 1) % X) * 2 + core
    right = ((x + 1) % X) * 2 + core
    far = ((x + 2) % X) * 2 + core
    low, high = pl.ds(0, ROWS // 2), pl.ds(ROWS // 2, ROWS // 2)

    def to(k, view, peer):
        return remote(view, view, x_send.at[k], x_recv.at[k], peer)

    own_up = to(0, out_ref.at[mine], x_up)
    own_down = to(1, out_ref.at[mine], x_down)
    own_mate = to(2, out_ref.at[mine], mate)
    start((own_up, own_down, own_mate))
    from_left = to(0, out_ref.at[left], x_up)
    from_right = to(1, out_ref.at[right], x_down)
    from_left.wait_recv()
    on_up = to(3, out_ref.at[left, low], x_up)
    left_mate = to(4, out_ref.at[left], mate)
    start((on_up, left_mate))
    from_right.wait_recv()
    on_down = to(5, out_ref.at[right, high], x_down)
    right_mate = to(6, out_ref.at[right], mate)
    start((on_down, right_mate))
    to(3, out_ref.at[far, low], x_up).wait_recv()
    to(5, out_ref.at[far, high], x_down).wait_recv()
    far_mate = to(7, out_ref.at[far], mate)
    far_mate.start()
    to(2, out_ref.at[x * 2 + 1 - core], mate).wait_recv()
    to(4, out_ref.at[((x + X - 1) % X) * 2 + 1 - core], mate).wait_recv()
    to(6, out_ref.at[((x + 1) % X) * 2 + 1 - core], mate).wait_recv()
    to(7, out_ref.at[((x + 2) % X) * 2 + 1 - core], mate).wait_recv()

    for copy in (own_up, own_down, own_mate, on_up, left_mate, on_down, right_mate, far_mate):
        copy.wait_send()
    for hop in range(4):
        for copy in q_copies(hop) + up(hop) + down(hop):
            copy.wait_send()
    for i in range(8):
        for copy in direct(i) + first_leg(i) + second_leg(i):
            copy.wait_send()


def project_kernel(heads_ref, weight_ref, expand_ref, out_ref):
    total = dot(heads_ref[0], weight_ref[pl.ds(0, LANES), :])
    for t in range(1, 8):
        total = total + dot(heads_ref[t], weight_ref[pl.ds(t * LANES, LANES), :])
    total = total.astype(jnp.bfloat16)
    for p in range(PROBLEMS):
        out_ref[p * SPAN : (p + 1) * SPAN, :] = dot(
            expand_ref[p], total[p * LIVE : (p + 1) * LIVE]
        ).astype(jnp.bfloat16)


def per_device(queries, step_kv, tile_kv, tile_slot, step_lengths, parents, out_weight):
    bf16, f32 = jnp.bfloat16, jnp.float32
    smem = pl.BlockSpec(memory_space=pltpu.SMEM)
    vmem = pl.BlockSpec(memory_space=pltpu.VMEM)
    hbm = pl.BlockSpec(memory_space=pl.ANY)
    weights = lax.all_gather(out_weight, "dp", axis=0, tiled=True)

    send, qt, mask, expand, meta = pl.pallas_call(
        prep_kernel,
        out_shape=(
            jax.ShapeDtypeStruct((Y, Z, 2, 2, TILE, HD), bf16),
            jax.ShapeDtypeStruct((PROBLEMS, HD, LANES), bf16),
            jax.ShapeDtypeStruct((PROBLEMS, SPAN, LIVE), f32),
            jax.ShapeDtypeStruct((PROBLEMS, SPAN, LIVE), bf16),
            jax.ShapeDtypeStruct((256,), jnp.int32),
        ),
        in_specs=[smem, smem, smem, vmem, hbm],
        out_specs=(hbm, vmem, vmem, vmem, smem),
        scratch_shapes=[
            pltpu.SMEM((32,), jnp.int32),
            pltpu.SMEM((32,), jnp.int32),
            pltpu.SMEM((64,), jnp.int32),
            pltpu.SemaphoreType.DMA((32,)),
        ],
        compiler_params=pltpu.CompilerParams(vmem_limit_bytes=16 * MIB),
        cost_estimate=pl.CostEstimate(flops=100_000_000, bytes_accessed=20_000_000, transcendentals=0),
        name="prep",
    )(tile_slot, step_lengths, parents, queries, tile_kv)

    heads = pl.pallas_call(
        plane_kernel,
        out_shape=jax.ShapeDtypeStruct((8, PROBLEMS * LIVE, LANES), bf16),
        in_specs=[smem, hbm, vmem, vmem, vmem],
        out_specs=vmem,
        scratch_shapes=[pltpu.VMEM((8, 2, TILE, HD), bf16)] * 8
        + [pltpu.VMEM((PROBLEMS, HD, LANES), bf16)] * 7
        + [
            pltpu.VMEM((8, 2, 2, TILE, HD), bf16),
            pltpu.VMEM((9, HD, LANES), f32),
            pltpu.VMEM((9, 1, LANES), f32),
            pltpu.VMEM((9, 1, LANES), f32),
            pltpu.VMEM((PROBLEMS, HD, LANES), f32),
            pltpu.VMEM((PROBLEMS, 1, LANES), f32),
            pltpu.VMEM((PROBLEMS, 1, LANES), f32),
        ]
        + [
            pltpu.VMEM((4, PROBLEMS, HD, LANES), bf16),
            pltpu.VMEM((4, 8, LANES), f32),
        ]
        * 4
        + [
            pltpu.SemaphoreType.DMA((8,)),
            pltpu.SemaphoreType.DMA((8, 6)),
            pltpu.SemaphoreType.DMA((8, 6)),
            pltpu.SemaphoreType.DMA((4, 2)),
            pltpu.SemaphoreType.DMA((4, 2)),
            pltpu.SemaphoreType.DMA((4, 2, 2)),
            pltpu.SemaphoreType.DMA((4, 2, 2)),
            pltpu.SemaphoreType.DMA((8,)),
            pltpu.SemaphoreType.DMA((8,)),
        ],
        compiler_params=pltpu.CompilerParams(
            collective_id=0, has_side_effects=True, vmem_limit_bytes=56 * MIB
        ),
        cost_estimate=pl.CostEstimate(
            flops=60_000_000_000, bytes_accessed=300_000_000, transcendentals=10_000_000
        ),
        name="planes",
    )(meta, send, qt, step_kv, mask)

    columns = out_weight.shape[1]
    block = 256
    return pl.pallas_call(
        project_kernel,
        out_shape=jax.ShapeDtypeStruct((PROBLEMS * SPAN, columns), bf16),
        grid=(columns // block,),
        in_specs=[
            pl.BlockSpec((8, PROBLEMS * LIVE, LANES), lambda i: (0, 0, 0)),
            pl.BlockSpec((4096, block), lambda i: (0, i)),
            pl.BlockSpec((PROBLEMS, SPAN, LIVE), lambda i: (0, 0, 0)),
        ],
        out_specs=pl.BlockSpec((PROBLEMS * SPAN, block), lambda i: (0, i)),
        compiler_params=pltpu.CompilerParams(vmem_limit_bytes=32 * MIB),
        cost_estimate=pl.CostEstimate(
            flops=4_400_000_000, bytes_accessed=14_000_000, transcendentals=0
        ),
        name="project",
    )(heads, weights, expand)


def solution(mesh):
    return jax.shard_map(
        per_device,
        mesh=mesh,
        in_specs=(
            P("dp", "tensor"),
            P(None, "dp", "tensor"),
            P(None, "dp", "tensor"),
            P(),
            P(),
            P(),
            P("dp", "tensor"),
        ),
        out_specs=P("dp", "tensor"),
        check_vma=False,
    )
```

```python
import functools
import math

import jax
import jax.numpy as jnp
from jax import lax
from jax.experimental import pallas as pl
from jax.experimental.pallas import tpu as pltpu
from jax.sharding import PartitionSpec as P

HD = 128
TILE = 256
STEPS = 8
STEP_LEN = 24
SPAN = STEPS * STEP_LEN
PROBLEMS = 4
GROUP = 4
LIVE = 128
LANES = GROUP * LIVE
Z = 8
Y = 4
X = 4
LOW = -1e30
SCALE = math.log2(math.e) / math.sqrt(HD)
MESH = pl.DeviceIdType.MESH
ORDER = (4, 3, 5, 2, 6, 1, 7, 0)
MIB = 1 << 20
VMEM = 60 * MIB
HALF = 512

META_ORDER = 0
META_OWNER = 64
META_SAME = 128
META_LAST = 192
META_SOURCE = 256


class Pair:
    def __init__(self, copy, leaving, arriving):
        self.start = lambda: copy(leaving).start()
        self.wait_send = lambda: copy(leaving).wait_send()
        self.wait_recv = lambda: copy(arriving).wait_recv()


def dot(a, b, dims=((1,), (0,))):
    return lax.dot_general(a, b, (dims, ((), ())), preferred_element_type=jnp.float32)


def prep_kernel(
    slot_hbm, length_hbm, parent_hbm, query_hbm,
    qt_ref, mask_ref, expand_ref, meta_ref,
    slot_ref, length_ref, parent_ref, query_ref, count, count_in, owner_of, sems,
):
    loads = [
        pltpu.make_async_copy(source, target, sems.at[i])
        for i, (source, target) in enumerate(
            (
                (slot_hbm, slot_ref),
                (length_hbm, length_ref),
                (parent_hbm, parent_ref),
                (query_hbm, query_ref),
            )
        )
    ]
    for load in loads:
        load.start()
    dp = lax.axis_index("dp")
    z, y = dp // Y, dp % Y

    def clear(i, _):
        count[i] = 0
        count_in[i] = 0
        return 0

    lax.fori_loop(0, 32, clear, 0)

    def clear_slots(i, _):
        owner_of[i] = -1
        meta_ref[META_ORDER + i] = 0
        meta_ref[META_OWNER + i] = 0
        meta_ref[META_SAME + i] = 0
        meta_ref[META_LAST + i] = 0
        meta_ref[META_SOURCE + i] = 0
        return 0

    lax.fori_loop(0, 64, clear_slots, 0)
    loads[0].wait()

    def place(t, _):
        d = slot_ref[dp * 32 + t] >> 2
        rz = ((d >> 2) - z) & 7
        r = ((d & 3) - y) & 3
        j = count[r * 8 + rz]
        count[r * 8 + rz] = j + 1
        meta_ref[META_SOURCE + rz * 8 + r * 2 + j] = t
        return 0

    lax.fori_loop(0, 32, place, 0)

    def arrive(q, _):
        s = slot_ref[z * 128 + q]
        d = s >> 2

        @pl.when((d & 3) == y)
        def _():
            rz = ((d >> 2) - z) & 7
            r = (y - (q >> 5)) & 3
            j = count_in[r * 8 + rz]
            count_in[r * 8 + rz] = j + 1
            owner_of[rz * 8 + r * 2 + j] = s & 3

        return 0

    lax.fori_loop(0, 128, arrive, 0)

    def arrange(i, n):
        rz, p = i // 4, i % 4
        n = jnp.where(p == 0, 0, n)

        def scan(s, carry):
            n, seen = carry
            match = owner_of[rz * 8 + s] == p

            @pl.when(match)
            def _():
                meta_ref[META_ORDER + rz * 8 + n] = s
                meta_ref[META_OWNER + rz * 8 + n] = p
                meta_ref[META_SAME + rz * 8 + n] = seen
                meta_ref[META_LAST + rz * 4 + p] = n + 1

            hit = match.astype(jnp.int32)
            return n + hit, jnp.maximum(seen, hit)

        n, _ = lax.fori_loop(0, 8, scan, (n, 0))
        return n

    lax.fori_loop(0, 32, arrange, 0)

    for load in loads[1:]:
        load.wait()
    row = lax.broadcasted_iota(jnp.int32, (SPAN, LIVE), 0)
    lane = lax.broadcasted_iota(jnp.int32, (SPAN, LIVE), 1)
    step_of = row // STEP_LEN
    position = row - step_of * STEP_LEN
    for p in range(PROBLEMS):
        problem = dp * PROBLEMS + p
        lengths = [length_ref[s, problem] for s in range(STEPS)]
        links = [parent_ref[s, problem] for s in range(STEPS)]
        starts, lines = [], []
        total = jnp.int32(0)
        for s in range(STEPS):
            starts.append(total)
            total = total + lengths[s]
            line = jnp.int32(1 << s)
            for b in range(s):
                line = line | jnp.where(links[s] == b, lines[b], 0)
            lines.append(line)
        row_start, row_length = jnp.zeros_like(row), jnp.zeros_like(row)
        row_bit = jnp.zeros_like(row)
        lane_step, lane_start, lane_line = jnp.zeros_like(row), jnp.zeros_like(row), jnp.zeros_like(row)
        for s in range(STEPS):
            here = step_of == s
            row_start = jnp.where(here, starts[s], row_start)
            row_length = jnp.where(here, lengths[s], row_length)
            row_bit = jnp.where(here, 1 << s, row_bit)
            passed = lane >= starts[s]
            lane_step = jnp.where(passed, s, lane_step)
            lane_start = jnp.where(passed, starts[s], lane_start)
            lane_line = jnp.where(passed, lines[s], lane_line)
        live = position < row_length
        picked = (lane == row_start + position) & live
        expand = jnp.where(picked, 1.0, 0.0).astype(jnp.bfloat16)
        expand_ref[p] = expand
        visible = (
            ((lane_line & row_bit) != 0)
            & live
            & ((step_of != lane_step) | (position <= lane - lane_start))
        )
        mask_ref[p] = jnp.where(visible, 1.0, 0.0)
        for h in range(GROUP):
            block = query_ref[p * SPAN : (p + 1) * SPAN, h * HD : (h + 1) * HD]
            qt_ref[p, :, h * LIVE : (h + 1) * LIVE] = dot(block, expand, ((0,), (0,))).astype(
                jnp.bfloat16
            )


def plane_kernel(
    meta_ref, qt_hbm, mask_hbm, step_hbm, tile_hbm, weight_hbm,
    out_ref,
    *scratch,
):
    tiles = scratch[0:8]
    qs = scratch[8:16]
    (
        mask_ref, step_ref, own_ref, send_ref, weights, heads,
        relay, state_o, state_m, state_l, step_o, step_m, step_l,
        up_in, up_in_s, up_out, up_out_s, down_in, down_in_s, down_out, down_out_s,
        own_sem, y_send, y_recv, q_send, q_recv, c_send, c_recv, x_send, x_recv, w_send, w_recv,
    ) = scratch[16:]
    dp, tensor = lax.axis_index("dp"), lax.axis_index("tensor")
    z, y = dp // Y, dp % Y
    x, core = tensor // 2, tensor % 2
    y_up = (z * Y + (y + 1) % Y, tensor)
    y_down = (z * Y + (y + Y - 1) % Y, tensor)
    z_up = (((z + 1) % Z) * Y + y, tensor)
    z_down = (((z + Z - 1) % Z) * Y + y, tensor)
    x_up = (dp, ((x + 1) % X) * 2 + core)
    x_down = (dp, ((x + X - 1) % X) * 2 + core)
    mate = (dp, x * 2 + 1 - core)

    loads = [
        pltpu.make_async_copy(source, target, own_sem.at[i])
        for i, (source, target) in enumerate(
            (
                (qt_hbm, qs[0]),
                (tile_hbm, own_ref),
                (weight_hbm.at[:, pl.ds(0, HALF)], weights.at[0, z, y]),
                (weight_hbm.at[:, pl.ds(HALF, HALF)], weights.at[1, z, y]),
                (step_hbm, step_ref),
                (mask_hbm, mask_ref),
            )
        )
    ]
    for load in loads:
        load.start()

    barrier = pltpu.get_barrier_semaphore()
    peers = (y_up, y_down, z_up, z_down, x_up, x_down, mate)
    for peer in peers:
        pl.semaphore_signal(barrier, inc=1, device_id=peer, device_id_type=MESH)
    pl.semaphore_wait(barrier, len(peers))

    def remote(src, dst, send_sem, recv_sem, peer):
        return pltpu.make_async_remote_copy(
            src_ref=src, dst_ref=dst, send_sem=send_sem, recv_sem=recv_sem,
            device_id=peer, device_id_type=MESH,
        )

    def q_copies(hop):
        up_from, up_to = (8 - hop) % 8, 7 - hop
        up_src, up_dst = qs[up_from], qs[up_to]
        down_src, down_dst = qs[hop], qs[hop + 1]
        if hop == 3:
            up_src, up_dst = up_src.at[pl.ds(0, 2)], up_dst.at[pl.ds(0, 2)]
            down_src, down_dst = down_src.at[pl.ds(2, 2)], down_dst.at[pl.ds(2, 2)]
        return (
            remote(up_src, up_dst, q_send.at[hop, 0], q_recv.at[hop, 0], z_up),
            remote(down_src, down_dst, q_send.at[hop, 1], q_recv.at[hop, 1], z_down),
        )

    def direct(i):
        rz = ORDER[i]
        return (
            remote(send_ref.at[i, pl.ds(0, 2)], tiles[rz].at[pl.ds(2, 2)], y_send.at[i, 0], y_recv.at[i, 0], y_up),
            remote(send_ref.at[i, pl.ds(4, 2)], tiles[rz].at[pl.ds(6, 2)], y_send.at[i, 1], y_recv.at[i, 1], y_down),
        )

    def first_leg(i):
        return (
            remote(send_ref.at[i, 2], relay.at[i, 0], y_send.at[i, 2], y_recv.at[i, 2], y_up),
            remote(send_ref.at[i, 3], relay.at[i, 1], y_send.at[i, 3], y_recv.at[i, 3], y_down),
        )

    def second_leg(i):
        rz = ORDER[i]
        return (
            remote(relay.at[i, 0], tiles[rz].at[4], y_send.at[i, 4], y_recv.at[i, 4], y_up),
            remote(relay.at[i, 1], tiles[rz].at[5], y_send.at[i, 5], y_recv.at[i, 5], y_down),
        )

    def pack(i):
        rz = ORDER[i]

        def keep(s, _):
            tiles[rz][s] = own_ref[:, meta_ref[META_SOURCE + rz * 8 + s]]
            return 0

        def give(s, _):
            send_ref[i, s] = own_ref[:, meta_ref[META_SOURCE + rz * 8 + 2 + s]]
            return 0

        lax.fori_loop(0, 2, keep, 0)
        lax.fori_loop(0, 6, give, 0)

    def along_z(view, low, high, k, hop):
        up_block, down_block = view((z + Z - hop) % Z), view((z + hop) % Z)
        up_next, down_next = view((z + Z - hop - 1) % Z), view((z + hop + 1) % Z)
        if hop == 3:
            up_block, up_next = up_block.at[low], up_next.at[low]
            down_block, down_next = down_block.at[high], down_next.at[high]
        return ring_pair(up_block, up_next, z_up, down_block, down_next, z_down, k + hop)

    def along_y(view, low, high, k, hop):
        up_block, down_block = view((y + Y - hop) % Y), view((y + hop) % Y)
        up_next, down_next = view((y + Y - hop - 1) % Y), view((y + hop + 1) % Y)
        if hop == 1:
            up_block, up_next = up_block.at[low], up_next.at[low]
            down_block, down_next = down_block.at[high], down_next.at[high]
        return ring_pair(up_block, up_next, y_up, down_block, down_next, y_down, k + hop)

    def ring_pair(up_block, up_next, up_peer, down_block, down_next, down_peer, k):
        def side(i, peer):
            return lambda block: remote(block, block, w_send.at[k, i], w_recv.at[k, i], peer)

        return (
            Pair(side(0, up_peer), up_block, up_next),
            Pair(side(1, down_peer), down_block, down_next),
        )

    first_rows, last_rows = pl.ds(0, HD // 2), pl.ds(HD // 2, HD // 2)

    def a1(hop):
        return along_y(lambda k: weights.at[0, z, k], first_rows, last_rows, 0, hop)

    def a2(hop):
        return along_z(lambda k: weights.at[0, k], pl.ds(0, 2), pl.ds(2, 2), 2, hop)

    def b1(hop):
        return along_z(lambda k: weights.at[1, k, y], first_rows, last_rows, 6, hop)

    def b2(hop):
        view = lambda k: weights.at[1, :, k]
        if hop == 0:
            return along_y(view, None, None, 10, 0)
        halves = pl.ds(0, 4), pl.ds(4, 4)
        up_block, down_block = weights.at[1, halves[0], (y + Y - 1) % Y], weights.at[1, halves[1], (y + 1) % Y]
        up_next, down_next = weights.at[1, halves[0], (y + 2) % Y], weights.at[1, halves[1], (y + 2) % Y]
        return ring_pair(up_block, up_next, y_up, down_block, down_next, y_down, 11)

    def start(copies):
        for copy in copies:
            copy.start()

    def arrived(copies):
        for copy in copies:
            copy.wait_recv()

    def pass_on(i):
        arrived(first_leg(i))
        start(second_leg(i))

    loads[0].wait()
    start(q_copies(0))
    loads[2].wait()
    loads[3].wait()
    start(a1(0))
    start(b1(0))
    loads[1].wait()
    for i in range(4):
        pack(i)
        start(first_leg(i))
        if i < 3:
            start(direct(i))

    state_o[0] = jnp.zeros((HD, LANES), jnp.float32)
    state_m[0] = jnp.full((1, LANES), LOW, jnp.float32)
    state_l[0] = jnp.zeros((1, LANES), jnp.float32)

    def soften(scores, m_before):
        m = jnp.maximum(m_before, jnp.max(scores, axis=0, keepdims=True))
        expo = jnp.exp2(scores - m)
        return m, jnp.sum(expo, axis=0, keepdims=True), expo.astype(jnp.bfloat16)

    def attend_steps(p, _):
        rows = pl.ds(pl.multiple_of(p * SPAN, SPAN), SPAN)
        mask = mask_ref[p]
        mask = jnp.concatenate([mask] * GROUP, axis=1)
        scores = dot(step_ref[0, rows, :], qs[0][p]) * SCALE
        scores = jnp.where(mask > 0.5, scores, LOW)
        m, l, weights = soften(scores, jnp.full((1, LANES), LOW, jnp.float32))
        step_o[p] = dot(step_ref[1, rows, :], weights, ((0,), (0,)))
        step_m[p] = m
        step_l[p] = l
        return 0

    def attend_tiles(rz):
        def one(s, _):
            slot = meta_ref[META_ORDER + rz * 8 + s]
            owner = meta_ref[META_OWNER + rz * 8 + s]
            same = meta_ref[META_SAME + rz * 8 + s]
            scores = dot(tiles[rz][slot, 0], qs[rz][owner]) * SCALE
            m_before = jnp.where(same > 0, state_m[s], LOW)
            m, l, weights = soften(scores, m_before)
            alpha = jnp.exp2(m_before - m)
            state_o[s + 1] = state_o[s] * alpha + dot(tiles[rz][slot, 1], weights, ((0,), (0,)))
            state_m[s + 1] = m
            state_l[s + 1] = state_l[s] * alpha + l
            return 0

        lax.fori_loop(0, 8, one, 0)

    def chain_copies(hop, out, out_s, inn, inn_s, side, peer):
        src, dst = out.at[hop], inn.at[hop]
        if hop == 0:
            half = pl.ds(2, 2) if side == 0 else pl.ds(0, 2)
            src, dst = out.at[hop, half], inn.at[hop, half]
        return (
            remote(src, dst, c_send.at[hop, side, 0], c_recv.at[hop, side, 0], peer),
            remote(out_s.at[hop], inn_s.at[hop], c_send.at[hop, side, 1], c_recv.at[hop, side, 1], peer),
        )

    def up(hop):
        return chain_copies(hop, up_out, up_out_s, up_in, up_in_s, 0, z_up)

    def down(hop):
        return chain_copies(hop, down_out, down_out_s, down_in, down_in_s, 1, z_down)

    def pass_sums(hop, rz, side):
        copies = (up, down)[side]
        out, out_s, inn, inn_s = (
            (up_out, up_out_s, up_in, up_in_s),
            (down_out, down_out_s, down_in, down_in_s),
        )[side]
        if hop > 0:
            arrived(copies(hop - 1))
        else:
            out_s[hop] = jnp.zeros((8, LANES), jnp.float32)

        def alone(p, _):
            last = meta_ref[META_LAST + rz * 4 + p]
            out[hop, p] = state_o[last].astype(jnp.bfloat16)
            out_s[hop, pl.ds(p, 1), :] = state_m[last]
            out_s[hop, pl.ds(p + 4, 1), :] = state_l[last]
            return 0

        def merged(p, _):
            last = meta_ref[META_LAST + rz * 4 + p]
            m_a, m_b = state_m[last], inn_s[hop - 1, pl.ds(p, 1), :]
            m = jnp.maximum(m_a, m_b)
            a, b = jnp.exp2(m_a - m), jnp.exp2(m_b - m)
            out[hop, p] = (state_o[last] * a + inn[hop - 1, p].astype(jnp.float32) * b).astype(
                jnp.bfloat16
            )
            out_s[hop, pl.ds(p, 1), :] = m
            out_s[hop, pl.ds(p + 4, 1), :] = (
                state_l[last] * a + inn_s[hop - 1, pl.ds(p + 4, 1), :] * b
            )
            return 0

        half = (2, 4) if side == 0 else (0, 2)
        other = (0, 2) if side == 0 else (2, 4)
        if hop == 0:
            lax.fori_loop(*half, alone, 0)
        elif hop == 1:
            lax.fori_loop(*half, merged, 0)
            lax.fori_loop(*other, alone, 0)
        else:
            lax.fori_loop(0, 4, merged, 0)
        start(copies(hop))

    for hop in range(3):
        arrived(q_copies(hop))
        start(q_copies(hop + 1))
        pass_on(hop)
        arrived(b1(hop))
        start(b1(hop + 1))
        if hop == 0:
            arrived(a1(0))
            start(a1(1))
    loads[4].wait()
    loads[5].wait()
    lax.fori_loop(0, PROBLEMS, attend_steps, 0)
    arrived(a1(1))

    for i in range(8):
        rz = ORDER[i]
        arrived(direct(i))
        arrived(second_leg(i))
        if i + 3 < 8:
            start(direct(i + 3))
            if i + 4 < 8:
                pack(i + 4)
                start(first_leg(i + 4))
            pass_on(i + 3)
        if i == 0:
            arrived(q_copies(3))
            arrived(b1(3))
            start(a2(0))
        if i == 5:
            start(b2(0))
        attend_tiles(rz)
        if rz == 4:
            pass_sums(0, rz, 0)
            pass_sums(0, rz, 1)
        elif rz in (3, 2, 1):
            pass_sums(4 - rz, rz, 0)
        elif rz in (5, 6, 7):
            pass_sums(rz - 4, rz, 1)
        if i in (2, 4, 6):
            arrived(a2(i // 2 - 1))
            start(a2(i // 2))
    arrived(up(3))
    arrived(down(3))

    mine = tensor

    def finish(p, _):
        last = meta_ref[META_LAST + p]
        terms = (
            (state_o[last], state_m[last], state_l[last]),
            (step_o[p], step_m[p], step_l[p]),
            (up_in[3, p].astype(jnp.float32), up_in_s[3, pl.ds(p, 1), :], up_in_s[3, pl.ds(p + 4, 1), :]),
            (down_in[3, p].astype(jnp.float32), down_in_s[3, pl.ds(p, 1), :], down_in_s[3, pl.ds(p + 4, 1), :]),
        )
        m = functools.reduce(jnp.maximum, [t[1] for t in terms])
        factors = [jnp.exp2(t[1] - m) for t in terms]
        total = sum(t[2] * f for t, f in zip(terms, factors))
        result = sum(t[0] * f for t, f in zip(terms, factors)) / total
        rows = pl.ds(pl.multiple_of(p * LIVE, LIVE), LIVE)
        for h in range(GROUP):
            block = result[:, h * LIVE : (h + 1) * LIVE]
            heads[mine, rows, h * HD : (h + 1) * HD] = block.T.astype(jnp.bfloat16)
        return 0

    lax.fori_loop(0, PROBLEMS, finish, 0)

    ROWS = PROBLEMS * LIVE
    left = ((x + X - 1) % X) * 2 + core
    right = ((x + 1) % X) * 2 + core
    far = ((x + 2) % X) * 2 + core
    low, high = pl.ds(0, ROWS // 2), pl.ds(ROWS // 2, ROWS // 2)

    def to(k, view, peer):
        return remote(view, view, x_send.at[k], x_recv.at[k], peer)

    own_up = to(0, heads.at[mine], x_up)
    own_down = to(1, heads.at[mine], x_down)
    own_mate = to(2, heads.at[mine], mate)
    start((own_up, own_down, own_mate))
    from_left = to(0, heads.at[left], x_up)
    from_right = to(1, heads.at[right], x_down)
    from_left.wait_recv()
    on_up = to(3, heads.at[left, low], x_up)
    left_mate = to(4, heads.at[left], mate)
    start((on_up, left_mate))
    from_right.wait_recv()
    on_down = to(5, heads.at[right, high], x_down)
    right_mate = to(6, heads.at[right], mate)
    start((on_down, right_mate))
    arrived(b2(0))
    start(b2(1))
    to(3, heads.at[far, low], x_up).wait_recv()
    to(5, heads.at[far, high], x_down).wait_recv()
    far_mate = to(7, heads.at[far], mate)
    far_mate.start()
    to(2, heads.at[x * 2 + 1 - core], mate).wait_recv()
    to(4, heads.at[((x + X - 1) % X) * 2 + 1 - core], mate).wait_recv()
    to(6, heads.at[((x + 1) % X) * 2 + 1 - core], mate).wait_recv()
    to(7, heads.at[((x + 2) % X) * 2 + 1 - core], mate).wait_recv()

    def project(half):
        def block(c, _):
            columns = pl.ds(pl.multiple_of(c * 256, 256), 256)
            total = jnp.zeros((ROWS, 256), jnp.float32)
            for t in range(8):
                block = weights[half, t, :, :, columns].reshape(LANES, 256)
                total = total + dot(heads[t], block)
            into = pl.ds(pl.multiple_of(half * HALF + c * 256, 256), 256)
            out_ref[:, into] = total.astype(jnp.bfloat16)
            return 0

        lax.fori_loop(0, HALF // 256, block, 0)

    arrived(a2(3))
    project(0)
    arrived(b2(1))
    project(1)

    for copy in (own_up, own_down, own_mate, on_up, left_mate, on_down, right_mate, far_mate):
        copy.wait_send()
    for hop in range(4):
        for copy in q_copies(hop) + up(hop) + down(hop):
            copy.wait_send()
        for copy in a2(hop) + b1(hop):
            copy.wait_send()
    for hop in range(2):
        for copy in a1(hop) + b2(hop):
            copy.wait_send()
    for i in range(8):
        for copy in direct(i) + first_leg(i) + second_leg(i):
            copy.wait_send()


def expand_kernel(compact_ref, expand_ref, out_ref):
    for p in range(PROBLEMS):
        out_ref[p * SPAN : (p + 1) * SPAN, :] = dot(
            expand_ref[p], compact_ref[p * LIVE : (p + 1) * LIVE, :]
        ).astype(jnp.bfloat16)


def per_device(queries, step_kv, tile_kv, tile_slot, step_lengths, parents, out_weight):
    bf16, f32, i32 = jnp.bfloat16, jnp.float32, jnp.int32
    smem = pl.BlockSpec(memory_space=pltpu.SMEM)
    vmem = pl.BlockSpec(memory_space=pltpu.VMEM)
    hbm = pl.BlockSpec(memory_space=pl.ANY)
    columns = out_weight.shape[1]

    qt, mask, expand, meta = pl.pallas_call(
        prep_kernel,
        out_shape=(
            jax.ShapeDtypeStruct((PROBLEMS, HD, LANES), bf16),
            jax.ShapeDtypeStruct((PROBLEMS, SPAN, LIVE), f32),
            jax.ShapeDtypeStruct((PROBLEMS, SPAN, LIVE), bf16),
            jax.ShapeDtypeStruct((512,), i32),
        ),
        in_specs=[hbm] * 4,
        out_specs=(vmem, vmem, vmem, smem),
        scratch_shapes=[
            pltpu.SMEM((1024,), i32),
            pltpu.SMEM((STEPS, 128), i32),
            pltpu.SMEM((STEPS, 128), i32),
            pltpu.VMEM(queries.shape, bf16),
            pltpu.SMEM((32,), i32),
            pltpu.SMEM((32,), i32),
            pltpu.SMEM((64,), i32),
            pltpu.SemaphoreType.DMA((4,)),
        ],
        compiler_params=pltpu.CompilerParams(vmem_limit_bytes=VMEM),
        cost_estimate=pl.CostEstimate(flops=100_000_000, bytes_accessed=4_000_000, transcendentals=0),
        name="prep",
    )(tile_slot, step_lengths.T, parents.T, queries)

    compact = pl.pallas_call(
        plane_kernel,
        out_shape=jax.ShapeDtypeStruct((PROBLEMS * LIVE, columns), bf16),
        in_specs=[smem] + [hbm] * 5,
        out_specs=vmem,
        scratch_shapes=[pltpu.VMEM((8, 2, TILE, HD), bf16)] * 8
        + [pltpu.VMEM((PROBLEMS, HD, LANES), bf16)] * 8
        + [
            pltpu.VMEM((PROBLEMS, SPAN, LIVE), f32),
            pltpu.VMEM(step_kv.shape, bf16),
            pltpu.VMEM((2, 32, TILE, HD), bf16),
            pltpu.VMEM((8, 6, 2, TILE, HD), bf16),
            pltpu.VMEM((2, Z, Y, HD, HALF), bf16),
            pltpu.VMEM((8, PROBLEMS * LIVE, LANES), bf16),
            pltpu.VMEM((8, 2, 2, TILE, HD), bf16),
            pltpu.VMEM((9, HD, LANES), f32),
            pltpu.VMEM((9, 1, LANES), f32),
            pltpu.VMEM((9, 1, LANES), f32),
            pltpu.VMEM((PROBLEMS, HD, LANES), f32),
            pltpu.VMEM((PROBLEMS, 1, LANES), f32),
            pltpu.VMEM((PROBLEMS, 1, LANES), f32),
        ]
        + [
            pltpu.VMEM((4, PROBLEMS, HD, LANES), bf16),
            pltpu.VMEM((4, 8, LANES), f32),
        ]
        * 4
        + [
            pltpu.SemaphoreType.DMA((8,)),
            pltpu.SemaphoreType.DMA((8, 6)),
            pltpu.SemaphoreType.DMA((8, 6)),
            pltpu.SemaphoreType.DMA((4, 2)),
            pltpu.SemaphoreType.DMA((4, 2)),
            pltpu.SemaphoreType.DMA((4, 2, 2)),
            pltpu.SemaphoreType.DMA((4, 2, 2)),
            pltpu.SemaphoreType.DMA((8,)),
            pltpu.SemaphoreType.DMA((8,)),
            pltpu.SemaphoreType.DMA((12, 2)),
            pltpu.SemaphoreType.DMA((12, 2)),
        ],
        compiler_params=pltpu.CompilerParams(
            collective_id=0, has_side_effects=True, vmem_limit_bytes=VMEM
        ),
        cost_estimate=pl.CostEstimate(
            flops=60_000_000_000, bytes_accessed=300_000_000, transcendentals=10_000_000
        ),
        name="planes",
    )(meta, qt, mask, step_kv, tile_kv.reshape(2, 32, TILE, HD), out_weight)

    block = 512
    return pl.pallas_call(
        expand_kernel,
        out_shape=jax.ShapeDtypeStruct((PROBLEMS * SPAN, columns), bf16),
        grid=(columns // block,),
        in_specs=[
            pl.BlockSpec((PROBLEMS * LIVE, block), lambda i: (0, i)),
            pl.BlockSpec((PROBLEMS, SPAN, LIVE), lambda i: (0, 0, 0)),
        ],
        out_specs=pl.BlockSpec((PROBLEMS * SPAN, block), lambda i: (0, i)),
        compiler_params=pltpu.CompilerParams(vmem_limit_bytes=VMEM),
        cost_estimate=pl.CostEstimate(
            flops=200_000_000, bytes_accessed=3_000_000, transcendentals=0
        ),
        name="expand",
    )(compact, expand)


def solution(mesh):
    return jax.shard_map(
        per_device,
        mesh=mesh,
        in_specs=(
            P("dp", "tensor"),
            P(None, "dp", "tensor"),
            P(None, "dp", "tensor"),
            P(),
            P(),
            P(),
            P("dp", "tensor"),
        ),
        out_specs=P("dp", "tensor"),
        check_vma=False,
    )
```

```python
import functools
import math

import jax
import jax.numpy as jnp
from jax import lax
from jax.experimental import pallas as pl
from jax.experimental.pallas import tpu as pltpu
from jax.sharding import PartitionSpec as P

HD = 128
TILE = 256
STEPS = 8
STEP_LEN = 24
SPAN = STEPS * STEP_LEN
PROBLEMS = 4
GROUP = 4
LIVE = 128
LANES = GROUP * LIVE
Z = 8
Y = 4
X = 4
LOW = -1e30
SCALE = math.log2(math.e) / math.sqrt(HD)
MESH = pl.DeviceIdType.MESH
ORDER = (4, 3, 5, 2, 6, 1, 7, 0)
MIB = 1 << 20
VMEM = 60 * MIB
PART_A = 256
PART_B = 768
HALVES = ((2, 4), (0, 2))
AHEAD = 4
B2_TURN = 3

META_ORDER = 0
META_OWNER = 64
META_SAME = 128
META_LAST = 192
META_SOURCE = 256
CAPACITIES = (12, 13, 16)


class Pair:
    def __init__(self, copy, leaving, arriving):
        self.start = lambda: copy(leaving).start()
        self.wait_send = lambda: copy(leaving).wait_send()
        self.wait_recv = lambda: copy(arriving).wait_recv()


def dot(a, b, dims=((1,), (0,))):
    return lax.dot_general(a, b, (dims, ((), ())), preferred_element_type=jnp.float32)


def prep_kernel(
    slot_hbm, table_hbm, length_hbm, parent_hbm, query_hbm,
    qt_ref, mask_ref, expand_ref, meta_ref, choice_ref,
    slot_ref, table_ref, length_ref, parent_ref, query_ref,
    count, count_in, rank, given, taken, place_of, sems,
):
    loads = [
        pltpu.make_async_copy(source, target, sems.at[i])
        for i, (source, target) in enumerate(
            (
                (slot_hbm, slot_ref),
                (table_hbm, table_ref),
                (length_hbm, length_ref),
                (parent_hbm, parent_ref),
                (query_hbm, query_ref),
            )
        )
    ]
    for load in loads:
        load.start()
    dp = lax.axis_index("dp")
    z, y = dp // Y, dp % Y

    def clear(i, _):
        count[i] = 0
        count_in[i] = 0
        return 0

    lax.fori_loop(0, 32, clear, 0)

    def clear_slots(i, _):
        given[i] = -1
        taken[i] = -1
        meta_ref[META_ORDER + i] = 0
        meta_ref[META_OWNER + i] = 0
        meta_ref[META_SAME + i] = 0
        meta_ref[META_LAST + i] = 0
        meta_ref[META_SOURCE + i] = 0
        return 0

    lax.fori_loop(0, 64, clear_slots, 0)
    for i, rz in enumerate(ORDER):
        rank[rz] = i
    loads[0].wait()

    def place(t, _):
        d = slot_ref[dp * 32 + t] >> 2
        turn = rank[((d >> 2) - z) & 7]
        r = ((d & 3) - y) & 3
        j = count[r * 8 + turn]
        count[r * 8 + turn] = j + 1
        given[r * 16 + turn * 2 + j] = t
        return 0

    lax.fori_loop(0, 32, place, 0)

    def arrive(q, _):
        s = slot_ref[z * 128 + q]
        d = s >> 2

        @pl.when((d & 3) == y)
        def _():
            turn = rank[((d >> 2) - z) & 7]
            r = (y - (q >> 5)) & 3
            j = count_in[r * 8 + turn]
            count_in[r * 8 + turn] = j + 1
            taken[r * 16 + turn * 2 + j] = s & 3

        return 0

    lax.fori_loop(0, 128, arrive, 0)

    def close(i, carry):
        sent, got = carry
        sent, got = jnp.where(i % 16 == 0, 0, sent), jnp.where(i % 16 == 0, 0, got)
        base = (i // 16) * 16
        tile = given[i]
        give, take = tile >= 0, taken[i] >= 0

        @pl.when(give)
        def _():
            meta_ref[META_SOURCE + base + sent] = tile

        place_of[i] = base + got
        return sent + give.astype(jnp.int32), got + take.astype(jnp.int32)

    lax.fori_loop(0, 64, close, (0, 0))

    def arrange(i, n):
        turn, p = i // 4, i % 4
        n = jnp.where(p == 0, 0, n)

        def scan(s, carry):
            n, seen = carry
            index = (s // 2) * 16 + turn * 2 + s % 2
            match = taken[index] == p

            @pl.when(match)
            def _():
                meta_ref[META_ORDER + turn * 8 + n] = place_of[index]
                meta_ref[META_OWNER + turn * 8 + n] = p
                meta_ref[META_SAME + turn * 8 + n] = seen
                meta_ref[META_LAST + turn * 4 + p] = n + 1

            hit = match.astype(jnp.int32)
            return n + hit, jnp.maximum(seen, hit)

        n, _ = lax.fori_loop(0, 8, scan, (n, 0))
        return n

    lax.fori_loop(0, 32, arrange, 0)

    for load in loads[1:]:
        load.wait()

    table = table_ref[...]
    column = (table >> 2) & 3
    lane = lax.broadcasted_iota(jnp.int32, (8, 128), 1) // 32
    block = lax.broadcasted_iota(jnp.int32, (128, 128), 0) // 32
    same_block = block == lax.broadcasted_iota(jnp.int32, (128, 128), 1) // 32
    ones = jnp.where(same_block, 1.0, 0.0).astype(jnp.bfloat16)
    most = jnp.zeros((8, 128), jnp.float32)
    for v in range(Y):
        hit = jnp.where((column == v) & (lane != v), 1.0, 0.0).astype(jnp.bfloat16)
        most = jnp.maximum(most, dot(hit, ones))
    most = jnp.max(most)
    choice = jnp.int32(0)
    for capacity in CAPACITIES[:-1]:
        choice = choice + (most > capacity + 0.5).astype(jnp.int32)
    choice_ref[0] = choice

    row = lax.broadcasted_iota(jnp.int32, (SPAN, LIVE), 0)
    lane = lax.broadcasted_iota(jnp.int32, (SPAN, LIVE), 1)
    step_of = row // STEP_LEN
    position = row - step_of * STEP_LEN
    for p in range(PROBLEMS):
        problem = dp * PROBLEMS + p
        lengths = [length_ref[s, problem] for s in range(STEPS)]
        links = [parent_ref[s, problem] for s in range(STEPS)]
        starts, lines = [], []
        total = jnp.int32(0)
        for s in range(STEPS):
            starts.append(total)
            total = total + lengths[s]
            line = jnp.int32(1 << s)
            for b in range(s):
                line = line | jnp.where(links[s] == b, lines[b], 0)
            lines.append(line)
        row_start, row_length = jnp.zeros_like(row), jnp.zeros_like(row)
        row_bit = jnp.zeros_like(row)
        lane_step, lane_start, lane_line = jnp.zeros_like(row), jnp.zeros_like(row), jnp.zeros_like(row)
        for s in range(STEPS):
            here = step_of == s
            row_start = jnp.where(here, starts[s], row_start)
            row_length = jnp.where(here, lengths[s], row_length)
            row_bit = jnp.where(here, 1 << s, row_bit)
            passed = lane >= starts[s]
            lane_step = jnp.where(passed, s, lane_step)
            lane_start = jnp.where(passed, starts[s], lane_start)
            lane_line = jnp.where(passed, lines[s], lane_line)
        live = position < row_length
        picked = (lane == row_start + position) & live
        expand = jnp.where(picked, 1.0, 0.0).astype(jnp.bfloat16)
        expand_ref[p] = expand
        visible = (
            ((lane_line & row_bit) != 0)
            & live
            & ((step_of != lane_step) | (position <= lane - lane_start))
        )
        mask_ref[p] = jnp.where(visible, 1.0, 0.0)
        for h in range(GROUP):
            block = query_ref[p * SPAN : (p + 1) * SPAN, h * HD : (h + 1) * HD]
            qt_ref[p, :, h * LIVE : (h + 1) * LIVE] = dot(block, expand, ((0,), (0,))).astype(
                jnp.bfloat16
            )


def plane_kernel(
    capacity,
    meta_ref, qt_hbm, mask_hbm, step_hbm, tile_hbm, weight_hbm,
    out_ref,
    *scratch,
):
    qs = scratch[0:8]
    (
        mask_ref, step_ref, own_ref, send_ref, here_ref, pool_ref, weights_a, weights_b, heads,
        relay, state_o, state_m, state_l, step_o, step_m, step_l,
        up_in, up_in_s, up_out, up_out_s, down_in, down_in_s, down_out, down_out_s,
        total_b, own_sem, y_send, y_recv, q_send, q_recv, c_send, c_recv, x_send, x_recv, w_send, w_recv,
    ) = scratch[8:]
    chunks = (capacity + 1) // 2
    dp, tensor = lax.axis_index("dp"), lax.axis_index("tensor")
    z, y = dp // Y, dp % Y
    x, core = tensor // 2, tensor % 2
    y_up = (z * Y + (y + 1) % Y, tensor)
    y_down = (z * Y + (y + Y - 1) % Y, tensor)
    z_up = (((z + 1) % Z) * Y + y, tensor)
    z_down = (((z + Z - 1) % Z) * Y + y, tensor)
    x_up = (dp, ((x + 1) % X) * 2 + core)
    x_down = (dp, ((x + X - 1) % X) * 2 + core)
    mate = (dp, x * 2 + 1 - core)

    loads = [
        pltpu.make_async_copy(source, target, own_sem.at[i])
        for i, (source, target) in enumerate(
            (
                (qt_hbm, qs[0]),
                (tile_hbm, own_ref),
                (weight_hbm.at[:, pl.ds(0, PART_A)], weights_a.at[z, y]),
                (weight_hbm.at[:, pl.ds(PART_A, PART_B)], weights_b.at[z, y]),
                (step_hbm, step_ref),
                (mask_hbm, mask_ref),
            )
        )
    ]
    for load in loads:
        load.start()

    barrier = pltpu.get_barrier_semaphore()
    peers = (y_up, y_down, z_up, z_down, x_up, x_down, mate)
    for peer in peers:
        pl.semaphore_signal(barrier, inc=1, device_id=peer, device_id_type=MESH)
    pl.semaphore_wait(barrier, len(peers))

    def remote(src, dst, send_sem, recv_sem, peer):
        return pltpu.make_async_remote_copy(
            src_ref=src, dst_ref=dst, send_sem=send_sem, recv_sem=recv_sem,
            device_id=peer, device_id_type=MESH,
        )

    def q_copies(hop):
        up_from, up_to = (8 - hop) % 8, 7 - hop
        up_src, up_dst = qs[up_from], qs[up_to]
        down_src, down_dst = qs[hop], qs[hop + 1]
        if hop == 3:
            up_src, up_dst = up_src.at[pl.ds(0, 2)], up_dst.at[pl.ds(0, 2)]
            down_src, down_dst = down_src.at[pl.ds(2, 2)], down_dst.at[pl.ds(2, 2)]
        return (
            remote(up_src, up_dst, q_send.at[hop, 0], q_recv.at[hop, 0], z_up),
            remote(down_src, down_dst, q_send.at[hop, 1], q_recv.at[hop, 1], z_down),
        )

    def span(i):
        return pl.ds(2 * i, min(2, capacity - 2 * i))

    def direct(i):
        at = span(i)
        return (
            remote(send_ref.at[0, at], here_ref.at[0, at], y_send.at[i, 0], y_recv.at[i, 0], y_up),
            remote(send_ref.at[2, at], here_ref.at[2, at], y_send.at[i, 1], y_recv.at[i, 1], y_down),
        )

    def first_leg(i):
        at = span(i)
        return (
            remote(send_ref.at[1, at, 0], relay.at[0, at], y_send.at[i, 2], y_recv.at[i, 2], y_up),
            remote(send_ref.at[1, at, 1], relay.at[1, at], y_send.at[i, 3], y_recv.at[i, 3], y_down),
        )

    def second_leg(i):
        at = span(i)
        return (
            remote(relay.at[0, at], here_ref.at[1, at, 0], y_send.at[i, 4], y_recv.at[i, 4], y_up),
            remote(relay.at[1, at], here_ref.at[1, at, 1], y_send.at[i, 5], y_recv.at[i, 5], y_down),
        )

    def pack(i):
        def give(k, _):
            for r in range(1, Y):
                send_ref[r - 1, k] = own_ref[:, meta_ref[META_SOURCE + r * 16 + k]]
            return 0

        lax.fori_loop(2 * i, min(2 * i + 2, capacity), give, 0)

    def keep(k, _):
        pool_ref[k] = own_ref[:, meta_ref[META_SOURCE + k]]
        return 0

    def join(i):
        arrived(direct(i))
        arrived(second_leg(i))
        for r in range(1, Y):
            for k in range(2 * i, min(2 * i + 2, capacity)):
                pool_ref[r * 16 + k] = here_ref[r - 1, k]

    def along_z(view, low, high, k, hop):
        up_block, down_block = view((z + Z - hop) % Z), view((z + hop) % Z)
        up_next, down_next = view((z + Z - hop - 1) % Z), view((z + hop + 1) % Z)
        if hop == 3:
            up_block, up_next = up_block.at[low], up_next.at[low]
            down_block, down_next = down_block.at[high], down_next.at[high]
        return ring_pair(up_block, up_next, z_up, down_block, down_next, z_down, k + hop)

    def along_y(view, low, high, k, hop):
        up_block, down_block = view((y + Y - hop) % Y), view((y + hop) % Y)
        up_next, down_next = view((y + Y - hop - 1) % Y), view((y + hop + 1) % Y)
        if hop == 1:
            up_block, up_next = up_block.at[low], up_next.at[low]
            down_block, down_next = down_block.at[high], down_next.at[high]
        return ring_pair(up_block, up_next, y_up, down_block, down_next, y_down, k + hop)

    def ring_pair(up_block, up_next, up_peer, down_block, down_next, down_peer, k):
        def side(i, peer):
            return lambda block: remote(block, block, w_send.at[k, i], w_recv.at[k, i], peer)

        return (
            Pair(side(0, up_peer), up_block, up_next),
            Pair(side(1, down_peer), down_block, down_next),
        )

    first_rows, last_rows = pl.ds(0, HD // 2), pl.ds(HD // 2, HD // 2)

    def a1(hop):
        return along_y(lambda k: weights_a.at[z, k], first_rows, last_rows, 0, hop)

    def a2(hop):
        return along_z(lambda k: weights_a.at[k], pl.ds(0, 2), pl.ds(2, 2), 2, hop)

    def b1(hop):
        return along_z(lambda k: weights_b.at[k, y], first_rows, last_rows, 6, hop)

    def planes_pair(k, distance):
        return weights_b.at[pl.ds(2 * k, 2), (y + distance) % Y]

    def b2_near(k):
        other = (k + 2) % 4
        return ring_pair(
            planes_pair(k, 0), planes_pair(k, 3), y_up,
            planes_pair(other, 0), planes_pair(other, 1), y_down, 10 + k,
        )

    def b2_far(k):
        return ring_pair(
            planes_pair(k, 3), planes_pair(k, 2), y_up,
            planes_pair(k + 2, 1), planes_pair(k + 2, 2), y_down, 14 + k,
        )

    def start(copies):
        for copy in copies:
            copy.start()

    def arrived(copies):
        for copy in copies:
            copy.wait_recv()

    def pass_on(i):
        arrived(first_leg(i))
        start(second_leg(i))

    loads[0].wait()
    start(q_copies(0))
    loads[2].wait()
    loads[3].wait()
    loads[1].wait()
    for i in range(AHEAD):
        pack(i)
        start(first_leg(i))
        start(direct(i))
        if i == 0:
            start(a1(0))
            start(b1(0))
    lax.fori_loop(0, 16, keep, 0)

    state_o[0] = jnp.zeros((HD, LANES), jnp.float32)
    state_m[0] = jnp.full((1, LANES), LOW, jnp.float32)
    state_l[0] = jnp.zeros((1, LANES), jnp.float32)

    def soften(scores, m_before):
        m = jnp.maximum(m_before, jnp.max(scores, axis=0, keepdims=True))
        expo = jnp.exp2(scores - m)
        return m, jnp.sum(expo, axis=0, keepdims=True), expo.astype(jnp.bfloat16)

    def attend_steps(p, _):
        rows = pl.ds(pl.multiple_of(p * SPAN, SPAN), SPAN)
        mask = mask_ref[p]
        mask = jnp.concatenate([mask] * GROUP, axis=1)
        scores = dot(step_ref[0, rows, :], qs[0][p]) * SCALE
        scores = jnp.where(mask > 0.5, scores, LOW)
        m, l, weights = soften(scores, jnp.full((1, LANES), LOW, jnp.float32))
        step_o[p] = dot(step_ref[1, rows, :], weights, ((0,), (0,)))
        step_m[p] = m
        step_l[p] = l
        return 0

    def attend_tiles(turn):
        queries = qs[ORDER[turn]]

        def one(s, _):
            slot = meta_ref[META_ORDER + turn * 8 + s]
            owner = meta_ref[META_OWNER + turn * 8 + s]
            same = meta_ref[META_SAME + turn * 8 + s]
            scores = dot(pool_ref[slot, 0], queries[owner]) * SCALE
            m_before = jnp.where(same > 0, state_m[s], LOW)
            m, l, weights = soften(scores, m_before)
            alpha = jnp.exp2(m_before - m)
            state_o[s + 1] = state_o[s] * alpha + dot(pool_ref[slot, 1], weights, ((0,), (0,)))
            state_m[s + 1] = m
            state_l[s + 1] = state_l[s] * alpha + l
            return 0

        lax.fori_loop(0, 8, one, 0)

    def sums(hop, p, side):
        out, out_s, inn, inn_s, peer = (
            (up_out, up_out_s, up_in, up_in_s, z_up),
            (down_out, down_out_s, down_in, down_in_s, z_down),
        )[side]
        return (
            remote(out.at[hop, p], inn.at[hop, p], c_send.at[hop, side, p, 0], c_recv.at[hop, side, p, 0], peer),
            remote(out_s.at[hop, p], inn_s.at[hop, p], c_send.at[hop, side, p, 1], c_recv.at[hop, side, p, 1], peer),
        )

    def pass_sums(hop, turn, side):
        out, out_s, inn, inn_s = (
            (up_out, up_out_s, up_in, up_in_s),
            (down_out, down_out_s, down_in, down_in_s),
        )[side]

        def alone(p, _):
            last = meta_ref[META_LAST + turn * 4 + p]
            out[hop, p] = state_o[last].astype(jnp.bfloat16)
            out_s[hop, p, :, 0:LANES] = state_m[last]
            out_s[hop, p, :, LANES:] = state_l[last]
            start(sums(hop, p, side))
            return 0

        def merged(p, _):
            last = meta_ref[META_LAST + turn * 4 + p]
            arrived(sums(hop - 1, p, side))
            m_a, m_b = state_m[last], inn_s[hop - 1, p, :, 0:LANES]
            m = jnp.maximum(m_a, m_b)
            a, b = jnp.exp2(m_a - m), jnp.exp2(m_b - m)
            out[hop, p] = (state_o[last] * a + inn[hop - 1, p].astype(jnp.float32) * b).astype(
                jnp.bfloat16
            )
            out_s[hop, p, :, 0:LANES] = m
            out_s[hop, p, :, LANES:] = state_l[last] * a + inn_s[hop - 1, p, :, LANES:] * b
            start(sums(hop, p, side))
            return 0

        half = HALVES[side]
        if hop == 0:
            lax.fori_loop(*half, alone, 0)
        elif hop == 1 and side == 0:
            lax.fori_loop(0, 2, alone, 0)
            lax.fori_loop(2, 4, merged, 0)
        elif hop == 1:
            lax.fori_loop(0, 2, merged, 0)
            lax.fori_loop(2, 4, alone, 0)
        else:
            lax.fori_loop(0, 4, merged, 0)

    for hop in range(3):
        arrived(q_copies(hop))
        start(q_copies(hop + 1))
        pass_on(hop)
        arrived(b1(hop))
        start(b1(hop + 1))
        if hop == 0:
            arrived(a1(0))
            start(a1(1))
    for i in range(3, AHEAD):
        pass_on(i)
    loads[4].wait()
    loads[5].wait()
    lax.fori_loop(0, PROBLEMS, attend_steps, 0)
    arrived(a1(1))

    legs = {
        0: [(b1, 3, None, 0)],
        6: [(None, 0, a2, 0)],
    }
    for i in range(8):
        rz = ORDER[i]
        if i < chunks:
            join(i)
        ahead = i + AHEAD
        if ahead < chunks:
            pack(ahead)
            start(first_leg(ahead))
            start(direct(ahead))
        if AHEAD <= ahead - 1 < chunks:
            pass_on(ahead - 1)
        if i == 0:
            arrived(q_copies(3))
        if i == B2_TURN:
            for k in range(4):
                start(b2_near(k))
        attend_tiles(i)
        if rz == 4:
            pass_sums(0, i, 0)
            pass_sums(0, i, 1)
        elif rz in (3, 2, 1):
            pass_sums(4 - rz, i, 0)
        elif rz in (5, 6, 7):
            pass_sums(rz - 4, i, 1)
        for before, hop, after, next_hop in legs.get(i, ()):
            if before is not None:
                arrived(before(hop))
            if after is not None:
                start(after(next_hop))
        if i == 6:
            arrived(b2_near(0))
            start(b2_far(0))
    mine = tensor

    def finish(p):
        arrived(sums(3, p, 0))
        arrived(sums(3, p, 1))
        last = meta_ref[META_LAST + 28 + p]
        terms = (
            (state_o[last], state_m[last], state_l[last]),
            (step_o[p], step_m[p], step_l[p]),
            (up_in[3, p].astype(jnp.float32), up_in_s[3, p, :, 0:LANES], up_in_s[3, p, :, LANES:]),
            (down_in[3, p].astype(jnp.float32), down_in_s[3, p, :, 0:LANES], down_in_s[3, p, :, LANES:]),
        )
        m = functools.reduce(jnp.maximum, [t[1] for t in terms])
        factors = [jnp.exp2(t[1] - m) for t in terms]
        total = sum(t[2] * f for t, f in zip(terms, factors))
        result = sum(t[0] * f for t, f in zip(terms, factors)) / total
        for h in range(GROUP):
            block = result[:, h * LIVE : (h + 1) * LIVE]
            heads[mine, p, :, h * HD : (h + 1) * HD] = block.T.astype(jnp.bfloat16)

    left, right, far = (x + X - 1) % X, (x + 1) % X, (x + 2) % X

    def to(k, p, owner, peer):
        view = heads.at[owner, p]
        return remote(view, view, x_send.at[k, p], x_recv.at[k, p], peer)

    def own_heads(p):
        return to(0, p, mine, x_up), to(1, p, mine, x_down), to(2, p, mine, mate)

    def next_heads(p):
        onward = to(3, p, left * 2 + core, x_up) if p < 2 else to(3, p, right * 2 + core, x_down)
        return onward, to(4, p, left * 2 + core, mate), to(5, p, right * 2 + core, mate)

    def near_heads(p):
        return to(0, p, left * 2 + core, x_up), to(1, p, right * 2 + core, x_down)

    def far_heads(p):
        return (to(3, p, far * 2 + core, x_up if p < 2 else x_down),)

    def last_heads(p):
        return (to(6, p, far * 2 + core, mate),)

    def mate_heads(p):
        other = 1 - core
        return (
            to(2, p, x * 2 + other, mate),
            to(4, p, left * 2 + other, mate),
            to(5, p, right * 2 + other, mate),
            to(6, p, far * 2 + other, mate),
        )

    for p in range(PROBLEMS):
        finish(p)
        start(own_heads(p))
        if p > 0:
            arrived(near_heads(p - 1))
            start(next_heads(p - 1))
        if p == 2:
            arrived(a2(0))
            start(a2(1))
            arrived(b2_near(1))
            start(b2_far(1))
    arrived(near_heads(3))
    start(next_heads(3))
    arrived(a2(1))
    start(a2(2))
    for p in range(PROBLEMS):
        arrived(far_heads(p))
        start(last_heads(p))
    arrived(a2(2))
    start(a2(3))
    for p in range(PROBLEMS):
        arrived(mate_heads(p))

    def product(weights, t, columns):
        block = weights[t, :, :, columns].reshape(LANES, 256)
        return dot(heads[t].reshape(PROBLEMS * LIVE, LANES), block)

    def part_b(planes, more):
        def block(c, _):
            columns = pl.ds(pl.multiple_of(c * 256, 256), 256)
            total = sum(product(weights_b, t, columns) for t in planes)
            into = pl.ds(pl.multiple_of(PART_A + c * 256, 256), 256)
            if more:
                total_b[:, columns] = total
            else:
                out_ref[:, into] = (total_b[:, columns] + total).astype(jnp.bfloat16)
            return 0

        lax.fori_loop(0, PART_B // 256, block, 0)

    for k in range(2, 4):
        arrived(b2_near(k))
    arrived(b2_far(0))
    part_b((0, 1, 4, 5), True)
    arrived(a2(3))
    total_a = sum(product(weights_a, t, pl.ds(0, PART_A)) for t in range(8))
    out_ref[:, 0:PART_A] = total_a.astype(jnp.bfloat16)
    arrived(b2_far(1))
    part_b((2, 3, 6, 7), False)

    for p in range(PROBLEMS):
        for copy in own_heads(p) + next_heads(p) + last_heads(p):
            copy.wait_send()
    for hop in range(4):
        for copy in q_copies(hop) + a2(hop) + b1(hop):
            copy.wait_send()
        for side in range(2):
            for p in range(*HALVES[side]) if hop == 0 else range(PROBLEMS):
                for copy in sums(hop, p, side):
                    copy.wait_send()
    for hop in range(2):
        for copy in a1(hop) + b2_far(hop):
            copy.wait_send()
    for k in range(4):
        for copy in b2_near(k):
            copy.wait_send()
    for i in range(chunks):
        for copy in direct(i) + first_leg(i) + second_leg(i):
            copy.wait_send()


def expand_kernel(compact_ref, expand_ref, out_ref):
    for p in range(PROBLEMS):
        out_ref[p * SPAN : (p + 1) * SPAN, :] = dot(
            expand_ref[p], compact_ref[p * LIVE : (p + 1) * LIVE, :]
        ).astype(jnp.bfloat16)


def per_device(queries, step_kv, tile_kv, tile_slot, step_lengths, parents, out_weight):
    bf16, f32, i32 = jnp.bfloat16, jnp.float32, jnp.int32
    smem = pl.BlockSpec(memory_space=pltpu.SMEM)
    vmem = pl.BlockSpec(memory_space=pltpu.VMEM)
    hbm = pl.BlockSpec(memory_space=pl.ANY)
    columns = out_weight.shape[1]

    qt, mask, expand, meta, choice = pl.pallas_call(
        prep_kernel,
        out_shape=(
            jax.ShapeDtypeStruct((PROBLEMS, HD, LANES), bf16),
            jax.ShapeDtypeStruct((PROBLEMS, SPAN, LIVE), f32),
            jax.ShapeDtypeStruct((PROBLEMS, SPAN, LIVE), bf16),
            jax.ShapeDtypeStruct((512,), i32),
            jax.ShapeDtypeStruct((1,), i32),
        ),
        in_specs=[hbm] * 5,
        out_specs=(vmem, vmem, vmem, smem, smem),
        scratch_shapes=[
            pltpu.SMEM((1024,), i32),
            pltpu.VMEM((8, 128), i32),
            pltpu.SMEM((STEPS, 128), i32),
            pltpu.SMEM((STEPS, 128), i32),
            pltpu.VMEM(queries.shape, bf16),
            pltpu.SMEM((32,), i32),
            pltpu.SMEM((32,), i32),
            pltpu.SMEM((8,), i32),
            pltpu.SMEM((64,), i32),
            pltpu.SMEM((64,), i32),
            pltpu.SMEM((64,), i32),
            pltpu.SemaphoreType.DMA((5,)),
        ],
        compiler_params=pltpu.CompilerParams(vmem_limit_bytes=VMEM),
        cost_estimate=pl.CostEstimate(flops=100_000_000, bytes_accessed=4_000_000, transcendentals=0),
        name="prep",
    )(tile_slot, tile_slot.reshape(8, 128), step_lengths.T, parents.T, queries)

    planes = lambda number, capacity: pl.pallas_call(
        functools.partial(plane_kernel, capacity),
        out_shape=jax.ShapeDtypeStruct((PROBLEMS * LIVE, columns), bf16),
        in_specs=[smem] + [hbm] * 5,
        out_specs=vmem,
        scratch_shapes=[pltpu.VMEM((PROBLEMS, HD, LANES), bf16)] * 8
        + [
            pltpu.VMEM((PROBLEMS, SPAN, LIVE), f32),
            pltpu.VMEM(step_kv.shape, bf16),
            pltpu.VMEM((2, 32, TILE, HD), bf16),
            pltpu.VMEM((3, capacity, 2, TILE, HD), bf16),
            pltpu.VMEM((3, capacity, 2, TILE, HD), bf16),
            pltpu.VMEM((64, 2, TILE, HD), bf16),
            pltpu.VMEM((Z, Y, HD, PART_A), bf16),
            pltpu.VMEM((Z, Y, HD, PART_B), bf16),
            pltpu.VMEM((8, PROBLEMS, LIVE, LANES), bf16),
            pltpu.VMEM((2, capacity, TILE, HD), bf16),
            pltpu.VMEM((9, HD, LANES), f32),
            pltpu.VMEM((9, 1, LANES), f32),
            pltpu.VMEM((9, 1, LANES), f32),
            pltpu.VMEM((PROBLEMS, HD, LANES), f32),
            pltpu.VMEM((PROBLEMS, 1, LANES), f32),
            pltpu.VMEM((PROBLEMS, 1, LANES), f32),
        ]
        + [
            pltpu.VMEM((4, PROBLEMS, HD, LANES), bf16),
            pltpu.VMEM((4, PROBLEMS, 1, 2 * LANES), f32),
        ]
        * 4
        + [
            pltpu.VMEM((PROBLEMS * LIVE, PART_B), f32),
            pltpu.SemaphoreType.DMA((8,)),
            pltpu.SemaphoreType.DMA((8, 6)),
            pltpu.SemaphoreType.DMA((8, 6)),
            pltpu.SemaphoreType.DMA((4, 2)),
            pltpu.SemaphoreType.DMA((4, 2)),
            pltpu.SemaphoreType.DMA((4, 2, 4, 2)),
            pltpu.SemaphoreType.DMA((4, 2, 4, 2)),
            pltpu.SemaphoreType.DMA((7, 4)),
            pltpu.SemaphoreType.DMA((7, 4)),
            pltpu.SemaphoreType.DMA((16, 2)),
            pltpu.SemaphoreType.DMA((16, 2)),
        ],
        compiler_params=pltpu.CompilerParams(
            collective_id=number, has_side_effects=True, vmem_limit_bytes=VMEM
        ),
        cost_estimate=pl.CostEstimate(
            flops=60_000_000_000, bytes_accessed=300_000_000, transcendentals=10_000_000
        ),
        name="planes",
    )
    compact = lax.switch(
        choice[0],
        [planes(number, capacity) for number, capacity in enumerate(CAPACITIES)],
        meta, qt, mask, step_kv, tile_kv.reshape(2, 32, TILE, HD), out_weight,
    )

    block = 512
    return pl.pallas_call(
        expand_kernel,
        out_shape=jax.ShapeDtypeStruct((PROBLEMS * SPAN, columns), bf16),
        grid=(columns // block,),
        in_specs=[
            pl.BlockSpec((PROBLEMS * LIVE, block), lambda i: (0, i)),
            pl.BlockSpec((PROBLEMS, SPAN, LIVE), lambda i: (0, 0, 0)),
        ],
        out_specs=pl.BlockSpec((PROBLEMS * SPAN, block), lambda i: (0, i)),
        compiler_params=pltpu.CompilerParams(vmem_limit_bytes=VMEM),
        cost_estimate=pl.CostEstimate(
            flops=200_000_000, bytes_accessed=3_000_000, transcendentals=0
        ),
        name="expand",
    )(compact, expand)


def solution(mesh):
    return jax.shard_map(
        per_device,
        mesh=mesh,
        in_specs=(
            P("dp", "tensor"),
            P(None, "dp", "tensor"),
            P(None, "dp", "tensor"),
            P(),
            P(),
            P(),
            P("dp", "tensor"),
        ),
        out_specs=P("dp", "tensor"),
        check_vma=False,
    )
```

```python
import functools
import math

import jax
import jax.numpy as jnp
from jax import lax
from jax.experimental import pallas as pl
from jax.experimental.pallas import tpu as pltpu
from jax.sharding import PartitionSpec as P

HD = 128
TILE = 256
STEPS = 8
STEP_LEN = 24
SPAN = STEPS * STEP_LEN
PROBLEMS = 4
GROUP = 4
LIVE = 128
LANES = GROUP * LIVE
Z = 8
Y = 4
X = 4
LOW = -1e30
SCALE = math.log2(math.e) / math.sqrt(HD)
MESH = pl.DeviceIdType.MESH
ORDER = (4, 3, 5, 2, 6, 1, 7, 0)
MIB = 1 << 20
VMEM = 60 * MIB
PART_A = 256
PART_B = 768
HALVES = ((2, 4), (0, 2))
AHEAD = 4
B2_TURN = 3

META_ORDER = 0
META_OWNER = 64
META_SAME = 128
META_LAST = 192
META_SOURCE = 256
CAPACITIES = (12, 13, 16)


class Pair:
    def __init__(self, copy, leaving, arriving):
        self.start = lambda: copy(leaving).start()
        self.wait_send = lambda: copy(leaving).wait_send()
        self.wait_recv = lambda: copy(arriving).wait_recv()


def dot(a, b, dims=((1,), (0,))):
    return lax.dot_general(a, b, (dims, ((), ())), preferred_element_type=jnp.float32)


def prep_kernel(
    slot_hbm, table_hbm, length_hbm, parent_hbm, query_hbm,
    qt_ref, mask_ref, expand_ref, meta_ref, choice_ref,
    slot_ref, table_ref, length_ref, parent_ref, query_ref,
    count, count_in, rank, given, taken, place_of, sems,
):
    loads = [
        pltpu.make_async_copy(source, target, sems.at[i])
        for i, (source, target) in enumerate(
            (
                (slot_hbm, slot_ref),
                (table_hbm, table_ref),
                (length_hbm, length_ref),
                (parent_hbm, parent_ref),
                (query_hbm, query_ref),
            )
        )
    ]
    for load in loads:
        load.start()
    dp = lax.axis_index("dp")
    z, y = dp // Y, dp % Y

    def clear(i, _):
        count[i] = 0
        count_in[i] = 0
        return 0

    lax.fori_loop(0, 32, clear, 0)

    def clear_slots(i, _):
        given[i] = -1
        taken[i] = -1
        meta_ref[META_ORDER + i] = 0
        meta_ref[META_OWNER + i] = 0
        meta_ref[META_SAME + i] = 0
        meta_ref[META_LAST + i] = 0
        meta_ref[META_SOURCE + i] = 0
        return 0

    lax.fori_loop(0, 64, clear_slots, 0, unroll=8)
    for i, rz in enumerate(ORDER):
        rank[rz] = i
    loads[0].wait()

    def place(t, _):
        d = slot_ref[dp * 32 + t] >> 2
        turn = rank[((d >> 2) - z) & 7]
        r = ((d & 3) - y) & 3
        j = count[r * 8 + turn]
        count[r * 8 + turn] = j + 1
        given[r * 16 + turn * 2 + j] = t
        return 0

    lax.fori_loop(0, 32, place, 0, unroll=4)

    def arrive(q, _):
        s = slot_ref[z * 128 + q]
        d = s >> 2

        @pl.when((d & 3) == y)
        def _():
            turn = rank[((d >> 2) - z) & 7]
            r = (y - (q >> 5)) & 3
            j = count_in[r * 8 + turn]
            count_in[r * 8 + turn] = j + 1
            taken[r * 16 + turn * 2 + j] = s & 3

        return 0

    lax.fori_loop(0, 128, arrive, 0, unroll=8)

    def close(i, carry):
        sent, got = carry
        sent, got = jnp.where(i % 16 == 0, 0, sent), jnp.where(i % 16 == 0, 0, got)
        base = (i // 16) * 16
        tile = given[i]
        give, take = tile >= 0, taken[i] >= 0

        @pl.when(give)
        def _():
            meta_ref[META_SOURCE + base + sent] = tile

        place_of[i] = base + got
        return sent + give.astype(jnp.int32), got + take.astype(jnp.int32)

    lax.fori_loop(0, 64, close, (0, 0), unroll=8)

    def arrange(i, n):
        turn, p = i // 4, i % 4
        n = jnp.where(p == 0, 0, n)

        def scan(s, carry):
            n, seen = carry
            index = (s // 2) * 16 + turn * 2 + s % 2
            match = taken[index] == p

            @pl.when(match)
            def _():
                meta_ref[META_ORDER + turn * 8 + n] = place_of[index]
                meta_ref[META_OWNER + turn * 8 + n] = p
                meta_ref[META_SAME + turn * 8 + n] = seen
                meta_ref[META_LAST + turn * 4 + p] = n + 1

            hit = match.astype(jnp.int32)
            return n + hit, jnp.maximum(seen, hit)

        n, _ = lax.fori_loop(0, 8, scan, (n, 0), unroll=True)
        return n

    lax.fori_loop(0, 32, arrange, 0)

    for load in loads[1:]:
        load.wait()

    table = table_ref[...]
    column = (table >> 2) & 3
    lane = lax.broadcasted_iota(jnp.int32, (8, 128), 1) // 32
    block = lax.broadcasted_iota(jnp.int32, (128, 128), 0) // 32
    same_block = block == lax.broadcasted_iota(jnp.int32, (128, 128), 1) // 32
    ones = jnp.where(same_block, 1.0, 0.0).astype(jnp.bfloat16)
    most = jnp.zeros((8, 128), jnp.float32)
    for v in range(Y):
        hit = jnp.where((column == v) & (lane != v), 1.0, 0.0).astype(jnp.bfloat16)
        most = jnp.maximum(most, dot(hit, ones))
    most = jnp.max(most)
    choice = jnp.int32(0)
    for capacity in CAPACITIES[:-1]:
        choice = choice + (most > capacity + 0.5).astype(jnp.int32)
    choice_ref[0] = choice

    row = lax.broadcasted_iota(jnp.int32, (SPAN, LIVE), 0)
    lane = lax.broadcasted_iota(jnp.int32, (SPAN, LIVE), 1)
    step_of = row // STEP_LEN
    position = row - step_of * STEP_LEN
    for p in range(PROBLEMS):
        problem = dp * PROBLEMS + p
        lengths = [length_ref[s, problem] for s in range(STEPS)]
        links = [parent_ref[s, problem] for s in range(STEPS)]
        starts, lines = [], []
        total = jnp.int32(0)
        for s in range(STEPS):
            starts.append(total)
            total = total + lengths[s]
            line = jnp.int32(1 << s)
            for b in range(s):
                line = line | jnp.where(links[s] == b, lines[b], 0)
            lines.append(line)
        row_start, row_length = jnp.zeros_like(row), jnp.zeros_like(row)
        row_bit = jnp.zeros_like(row)
        lane_step, lane_start, lane_line = jnp.zeros_like(row), jnp.zeros_like(row), jnp.zeros_like(row)
        for s in range(STEPS):
            here = step_of == s
            row_start = jnp.where(here, starts[s], row_start)
            row_length = jnp.where(here, lengths[s], row_length)
            row_bit = jnp.where(here, 1 << s, row_bit)
            passed = lane >= starts[s]
            lane_step = jnp.where(passed, s, lane_step)
            lane_start = jnp.where(passed, starts[s], lane_start)
            lane_line = jnp.where(passed, lines[s], lane_line)
        live = position < row_length
        picked = (lane == row_start + position) & live
        expand = jnp.where(picked, 1.0, 0.0).astype(jnp.bfloat16)
        expand_ref[p] = expand
        visible = (
            ((lane_line & row_bit) != 0)
            & live
            & ((step_of != lane_step) | (position <= lane - lane_start))
        )
        mask_ref[p] = jnp.where(visible, 1.0, 0.0)
        for h in range(GROUP):
            block = query_ref[p * SPAN : (p + 1) * SPAN, h * HD : (h + 1) * HD]
            qt_ref[p, :, h * LIVE : (h + 1) * LIVE] = dot(block, expand, ((0,), (0,))).astype(
                jnp.bfloat16
            )


def plane_kernel(
    capacity,
    meta_ref, qt_hbm, mask_hbm, step_hbm, tile_hbm, weight_hbm,
    out_ref,
    *scratch,
):
    qs = scratch[0:8]
    (
        mask_ref, step_ref, own_ref, send_ref, here_ref, pool_ref, weights_a, weights_b, heads,
        relay, state_o, state_m, state_l, step_o, step_m, step_l,
        up_in, up_in_s, up_out, up_out_s, down_in, down_in_s, down_out, down_out_s,
        total_b, own_sem, y_send, y_recv, q_send, q_recv, c_send, c_recv, x_send, x_recv, w_send, w_recv,
    ) = scratch[8:]
    chunks = (capacity + 1) // 2
    dp, tensor = lax.axis_index("dp"), lax.axis_index("tensor")
    z, y = dp // Y, dp % Y
    x, core = tensor // 2, tensor % 2
    y_up = (z * Y + (y + 1) % Y, tensor)
    y_down = (z * Y + (y + Y - 1) % Y, tensor)
    z_up = (((z + 1) % Z) * Y + y, tensor)
    z_down = (((z + Z - 1) % Z) * Y + y, tensor)
    x_up = (dp, ((x + 1) % X) * 2 + core)
    x_down = (dp, ((x + X - 1) % X) * 2 + core)
    mate = (dp, x * 2 + 1 - core)

    loads = [
        pltpu.make_async_copy(source, target, own_sem.at[i])
        for i, (source, target) in enumerate(
            (
                (qt_hbm, qs[0]),
                (tile_hbm, own_ref),
                (weight_hbm.at[:, pl.ds(0, PART_A)], weights_a.at[z, y]),
                (weight_hbm.at[:, pl.ds(PART_A, PART_B)], weights_b.at[z, y]),
                (step_hbm, step_ref),
                (mask_hbm, mask_ref),
            )
        )
    ]
    for load in loads:
        load.start()

    barrier = pltpu.get_barrier_semaphore()
    peers = (y_up, y_down, z_up, z_down, x_up, x_down, mate)
    for peer in peers:
        pl.semaphore_signal(barrier, inc=1, device_id=peer, device_id_type=MESH)
    pl.semaphore_wait(barrier, len(peers))

    def remote(src, dst, send_sem, recv_sem, peer):
        return pltpu.make_async_remote_copy(
            src_ref=src, dst_ref=dst, send_sem=send_sem, recv_sem=recv_sem,
            device_id=peer, device_id_type=MESH,
        )

    def q_copies(hop):
        up_from, up_to = (8 - hop) % 8, 7 - hop
        up_src, up_dst = qs[up_from], qs[up_to]
        down_src, down_dst = qs[hop], qs[hop + 1]
        if hop == 3:
            up_src, up_dst = up_src.at[pl.ds(0, 2)], up_dst.at[pl.ds(0, 2)]
            down_src, down_dst = down_src.at[pl.ds(2, 2)], down_dst.at[pl.ds(2, 2)]
        return (
            remote(up_src, up_dst, q_send.at[hop, 0], q_recv.at[hop, 0], z_up),
            remote(down_src, down_dst, q_send.at[hop, 1], q_recv.at[hop, 1], z_down),
        )

    def span(i):
        return pl.ds(2 * i, min(2, capacity - 2 * i))

    def direct(i):
        at = span(i)
        return (
            remote(send_ref.at[0, at], here_ref.at[0, at], y_send.at[i, 0], y_recv.at[i, 0], y_up),
            remote(send_ref.at[2, at], here_ref.at[2, at], y_send.at[i, 1], y_recv.at[i, 1], y_down),
        )

    def first_leg(i):
        at = span(i)
        return (
            remote(send_ref.at[1, at, 0], relay.at[0, at], y_send.at[i, 2], y_recv.at[i, 2], y_up),
            remote(send_ref.at[1, at, 1], relay.at[1, at], y_send.at[i, 3], y_recv.at[i, 3], y_down),
        )

    def second_leg(i):
        at = span(i)
        return (
            remote(relay.at[0, at], here_ref.at[1, at, 0], y_send.at[i, 4], y_recv.at[i, 4], y_up),
            remote(relay.at[1, at], here_ref.at[1, at, 1], y_send.at[i, 5], y_recv.at[i, 5], y_down),
        )

    def pack(i):
        def give(k, _):
            for r in range(1, Y):
                send_ref[r - 1, k] = own_ref[:, meta_ref[META_SOURCE + r * 16 + k]]
            return 0

        lax.fori_loop(2 * i, min(2 * i + 2, capacity), give, 0)

    def keep(k, _):
        pool_ref[k] = own_ref[:, meta_ref[META_SOURCE + k]]
        return 0

    def join(i):
        arrived(direct(i))
        arrived(second_leg(i))
        for r in range(1, Y):
            for k in range(2 * i, min(2 * i + 2, capacity)):
                pool_ref[r * 16 + k] = here_ref[r - 1, k]

    def along_z(view, low, high, k, hop):
        up_block, down_block = view((z + Z - hop) % Z), view((z + hop) % Z)
        up_next, down_next = view((z + Z - hop - 1) % Z), view((z + hop + 1) % Z)
        if hop == 3:
            up_block, up_next = up_block.at[low], up_next.at[low]
            down_block, down_next = down_block.at[high], down_next.at[high]
        return ring_pair(up_block, up_next, z_up, down_block, down_next, z_down, k + hop)

    def along_y(view, low, high, k, hop):
        up_block, down_block = view((y + Y - hop) % Y), view((y + hop) % Y)
        up_next, down_next = view((y + Y - hop - 1) % Y), view((y + hop + 1) % Y)
        if hop == 1:
            up_block, up_next = up_block.at[low], up_next.at[low]
            down_block, down_next = down_block.at[high], down_next.at[high]
        return ring_pair(up_block, up_next, y_up, down_block, down_next, y_down, k + hop)

    def ring_pair(up_block, up_next, up_peer, down_block, down_next, down_peer, k):
        def side(i, peer):
            return lambda block: remote(block, block, w_send.at[k, i], w_recv.at[k, i], peer)

        return (
            Pair(side(0, up_peer), up_block, up_next),
            Pair(side(1, down_peer), down_block, down_next),
        )

    first_rows, last_rows = pl.ds(0, HD // 2), pl.ds(HD // 2, HD // 2)

    def a1(hop):
        return along_y(lambda k: weights_a.at[z, k], first_rows, last_rows, 0, hop)

    def a2(hop):
        return along_z(lambda k: weights_a.at[k], pl.ds(0, 2), pl.ds(2, 2), 2, hop)

    def b1(hop):
        return along_z(lambda k: weights_b.at[k, y], first_rows, last_rows, 6, hop)

    def planes_pair(k, distance):
        return weights_b.at[pl.ds(2 * k, 2), (y + distance) % Y]

    def b2_near(k):
        other = (k + 2) % 4
        return ring_pair(
            planes_pair(k, 0), planes_pair(k, 3), y_up,
            planes_pair(other, 0), planes_pair(other, 1), y_down, 10 + k,
        )

    def b2_far(k):
        return ring_pair(
            planes_pair(k, 3), planes_pair(k, 2), y_up,
            planes_pair(k + 2, 1), planes_pair(k + 2, 2), y_down, 14 + k,
        )

    def start(copies):
        for copy in copies:
            copy.start()

    def arrived(copies):
        for copy in copies:
            copy.wait_recv()

    def pass_on(i):
        arrived(first_leg(i))
        start(second_leg(i))

    loads[0].wait()
    start(q_copies(0))
    loads[2].wait()
    loads[3].wait()
    loads[1].wait()
    for i in range(AHEAD):
        pack(i)
        start(first_leg(i))
        start(direct(i))
        if i == 0:
            start(a1(0))
            start(b1(0))
    lax.fori_loop(0, 16, keep, 0)

    state_o[0] = jnp.zeros((HD, LANES), jnp.float32)
    state_m[0] = jnp.full((1, LANES), LOW, jnp.float32)
    state_l[0] = jnp.zeros((1, LANES), jnp.float32)

    def soften(scores, m_before):
        m = jnp.maximum(m_before, jnp.max(scores, axis=0, keepdims=True))
        expo = jnp.exp2(scores - m)
        return m, jnp.sum(expo, axis=0, keepdims=True), expo.astype(jnp.bfloat16)

    def attend_steps(p, _):
        rows = pl.ds(pl.multiple_of(p * SPAN, SPAN), SPAN)
        mask = mask_ref[p]
        mask = jnp.concatenate([mask] * GROUP, axis=1)
        scores = dot(step_ref[0, rows, :], qs[0][p]) * SCALE
        scores = jnp.where(mask > 0.5, scores, LOW)
        m, l, weights = soften(scores, jnp.full((1, LANES), LOW, jnp.float32))
        step_o[p] = dot(step_ref[1, rows, :], weights, ((0,), (0,)))
        step_m[p] = m
        step_l[p] = l
        return 0

    def attend_tiles(turn):
        queries = qs[ORDER[turn]]

        def one(s, _):
            slot = meta_ref[META_ORDER + turn * 8 + s]
            owner = meta_ref[META_OWNER + turn * 8 + s]
            same = meta_ref[META_SAME + turn * 8 + s]
            scores = dot(pool_ref[slot, 0], queries[owner]) * SCALE
            m_before = jnp.where(same > 0, state_m[s], LOW)
            m, l, weights = soften(scores, m_before)
            alpha = jnp.exp2(m_before - m)
            state_o[s + 1] = state_o[s] * alpha + dot(pool_ref[slot, 1], weights, ((0,), (0,)))
            state_m[s + 1] = m
            state_l[s + 1] = state_l[s] * alpha + l
            return 0

        lax.fori_loop(0, 8, one, 0, unroll=2)

    def sums(hop, p, side):
        out, out_s, inn, inn_s, peer = (
            (up_out, up_out_s, up_in, up_in_s, z_up),
            (down_out, down_out_s, down_in, down_in_s, z_down),
        )[side]
        return (
            remote(out.at[hop, p], inn.at[hop, p], c_send.at[hop, side, p, 0], c_recv.at[hop, side, p, 0], peer),
            remote(out_s.at[hop, p], inn_s.at[hop, p], c_send.at[hop, side, p, 1], c_recv.at[hop, side, p, 1], peer),
        )

    def pass_sums(hop, turn, side):
        out, out_s, inn, inn_s = (
            (up_out, up_out_s, up_in, up_in_s),
            (down_out, down_out_s, down_in, down_in_s),
        )[side]

        def alone(p, _):
            last = meta_ref[META_LAST + turn * 4 + p]
            out[hop, p] = state_o[last].astype(jnp.bfloat16)
            out_s[hop, p, :, 0:LANES] = state_m[last]
            out_s[hop, p, :, LANES:] = state_l[last]
            start(sums(hop, p, side))
            return 0

        def merged(p, _):
            last = meta_ref[META_LAST + turn * 4 + p]
            arrived(sums(hop - 1, p, side))
            m_a, m_b = state_m[last], inn_s[hop - 1, p, :, 0:LANES]
            m = jnp.maximum(m_a, m_b)
            a, b = jnp.exp2(m_a - m), jnp.exp2(m_b - m)
            out[hop, p] = (state_o[last] * a + inn[hop - 1, p].astype(jnp.float32) * b).astype(
                jnp.bfloat16
            )
            out_s[hop, p, :, 0:LANES] = m
            out_s[hop, p, :, LANES:] = state_l[last] * a + inn_s[hop - 1, p, :, LANES:] * b
            start(sums(hop, p, side))
            return 0

        half = HALVES[side]
        if hop == 0:
            lax.fori_loop(*half, alone, 0)
        elif hop == 1 and side == 0:
            lax.fori_loop(0, 2, alone, 0)
            lax.fori_loop(2, 4, merged, 0)
        elif hop == 1:
            lax.fori_loop(0, 2, merged, 0)
            lax.fori_loop(2, 4, alone, 0)
        else:
            lax.fori_loop(0, 4, merged, 0)

    for hop in range(3):
        arrived(q_copies(hop))
        start(q_copies(hop + 1))
        pass_on(hop)
        arrived(b1(hop))
        start(b1(hop + 1))
        if hop == 0:
            arrived(a1(0))
            start(a1(1))
    for i in range(3, AHEAD):
        pass_on(i)
    loads[4].wait()
    loads[5].wait()
    lax.fori_loop(0, PROBLEMS, attend_steps, 0)
    arrived(a1(1))

    legs = {
        0: [(b1, 3, None, 0)],
        6: [(None, 0, a2, 0)],
    }
    for i in range(8):
        rz = ORDER[i]
        if i < chunks:
            join(i)
        ahead = i + AHEAD
        if ahead < chunks:
            pack(ahead)
            start(first_leg(ahead))
            start(direct(ahead))
        if AHEAD <= ahead - 1 < chunks:
            pass_on(ahead - 1)
        if i == 0:
            arrived(q_copies(3))
        if i == B2_TURN:
            for k in range(4):
                start(b2_near(k))
        attend_tiles(i)
        if rz == 4:
            pass_sums(0, i, 0)
            pass_sums(0, i, 1)
        elif rz in (3, 2, 1):
            pass_sums(4 - rz, i, 0)
        elif rz in (5, 6, 7):
            pass_sums(rz - 4, i, 1)
        for before, hop, after, next_hop in legs.get(i, ()):
            if before is not None:
                arrived(before(hop))
            if after is not None:
                start(after(next_hop))
        if i == 6:
            arrived(b2_near(0))
            start(b2_far(0))
    mine = tensor

    def finish(p):
        arrived(sums(3, p, 0))
        arrived(sums(3, p, 1))
        last = meta_ref[META_LAST + 28 + p]
        terms = (
            (state_o[last], state_m[last], state_l[last]),
            (step_o[p], step_m[p], step_l[p]),
            (up_in[3, p].astype(jnp.float32), up_in_s[3, p, :, 0:LANES], up_in_s[3, p, :, LANES:]),
            (down_in[3, p].astype(jnp.float32), down_in_s[3, p, :, 0:LANES], down_in_s[3, p, :, LANES:]),
        )
        m = functools.reduce(jnp.maximum, [t[1] for t in terms])
        factors = [jnp.exp2(t[1] - m) for t in terms]
        total = sum(t[2] * f for t, f in zip(terms, factors))
        result = sum(t[0] * f for t, f in zip(terms, factors)) / total
        for h in range(GROUP):
            block = result[:, h * LIVE : (h + 1) * LIVE]
            heads[mine, p, :, h * HD : (h + 1) * HD] = block.T.astype(jnp.bfloat16)

    left, right, far = (x + X - 1) % X, (x + 1) % X, (x + 2) % X

    def to(k, p, owner, peer):
        view = heads.at[owner, p]
        return remote(view, view, x_send.at[k, p], x_recv.at[k, p], peer)

    def own_heads(p):
        return to(0, p, mine, x_up), to(1, p, mine, x_down), to(2, p, mine, mate)

    def next_heads(p):
        onward = to(3, p, left * 2 + core, x_up) if p < 2 else to(3, p, right * 2 + core, x_down)
        return onward, to(4, p, left * 2 + core, mate), to(5, p, right * 2 + core, mate)

    def near_heads(p):
        return to(0, p, left * 2 + core, x_up), to(1, p, right * 2 + core, x_down)

    def far_heads(p):
        return (to(3, p, far * 2 + core, x_up if p < 2 else x_down),)

    def last_heads(p):
        return (to(6, p, far * 2 + core, mate),)

    def mate_heads(p):
        other = 1 - core
        return (
            to(2, p, x * 2 + other, mate),
            to(4, p, left * 2 + other, mate),
            to(5, p, right * 2 + other, mate),
            to(6, p, far * 2 + other, mate),
        )

    for p in range(PROBLEMS):
        finish(p)
        start(own_heads(p))
        if p > 0:
            arrived(near_heads(p - 1))
            start(next_heads(p - 1))
        if p == 2:
            arrived(a2(0))
            start(a2(1))
            arrived(b2_near(1))
            start(b2_far(1))
    arrived(near_heads(3))
    start(next_heads(3))
    arrived(a2(1))
    start(a2(2))
    for p in range(PROBLEMS):
        arrived(far_heads(p))
        start(last_heads(p))
    arrived(a2(2))
    start(a2(3))
    for p in range(PROBLEMS):
        arrived(mate_heads(p))

    def product(weights, t, columns):
        block = weights[t, :, :, columns].reshape(LANES, 256)
        return dot(heads[t].reshape(PROBLEMS * LIVE, LANES), block)

    def part_b(planes, more):
        def block(c, _):
            columns = pl.ds(pl.multiple_of(c * 256, 256), 256)
            total = sum(product(weights_b, t, columns) for t in planes)
            into = pl.ds(pl.multiple_of(PART_A + c * 256, 256), 256)
            if more:
                total_b[:, columns] = total
            else:
                out_ref[:, into] = (total_b[:, columns] + total).astype(jnp.bfloat16)
            return 0

        lax.fori_loop(0, PART_B // 256, block, 0)

    for k in range(2, 4):
        arrived(b2_near(k))
    arrived(b2_far(0))
    part_b((0, 1, 4, 5), True)
    arrived(a2(3))
    total_a = sum(product(weights_a, t, pl.ds(0, PART_A)) for t in range(8))
    out_ref[:, 0:PART_A] = total_a.astype(jnp.bfloat16)
    arrived(b2_far(1))
    part_b((2, 3, 6, 7), False)

    for p in range(PROBLEMS):
        for copy in own_heads(p) + next_heads(p) + last_heads(p):
            copy.wait_send()
    for hop in range(4):
        for copy in q_copies(hop) + a2(hop) + b1(hop):
            copy.wait_send()
        for side in range(2):
            for p in range(*HALVES[side]) if hop == 0 else range(PROBLEMS):
                for copy in sums(hop, p, side):
                    copy.wait_send()
    for hop in range(2):
        for copy in a1(hop) + b2_far(hop):
            copy.wait_send()
    for k in range(4):
        for copy in b2_near(k):
            copy.wait_send()
    for i in range(chunks):
        for copy in direct(i) + first_leg(i) + second_leg(i):
            copy.wait_send()


def expand_kernel(compact_ref, expand_ref, out_ref):
    for p in range(PROBLEMS):
        out_ref[p * SPAN : (p + 1) * SPAN, :] = dot(
            expand_ref[p], compact_ref[p * LIVE : (p + 1) * LIVE, :]
        ).astype(jnp.bfloat16)


def per_device(queries, step_kv, tile_kv, tile_slot, step_lengths, parents, out_weight):
    bf16, f32, i32 = jnp.bfloat16, jnp.float32, jnp.int32
    smem = pl.BlockSpec(memory_space=pltpu.SMEM)
    vmem = pl.BlockSpec(memory_space=pltpu.VMEM)
    hbm = pl.BlockSpec(memory_space=pl.ANY)
    columns = out_weight.shape[1]

    qt, mask, expand, meta, choice = pl.pallas_call(
        prep_kernel,
        out_shape=(
            jax.ShapeDtypeStruct((PROBLEMS, HD, LANES), bf16),
            jax.ShapeDtypeStruct((PROBLEMS, SPAN, LIVE), f32),
            jax.ShapeDtypeStruct((PROBLEMS, SPAN, LIVE), bf16),
            jax.ShapeDtypeStruct((512,), i32),
            jax.ShapeDtypeStruct((1,), i32),
        ),
        in_specs=[hbm] * 5,
        out_specs=(vmem, vmem, vmem, smem, smem),
        scratch_shapes=[
            pltpu.SMEM((1024,), i32),
            pltpu.VMEM((8, 128), i32),
            pltpu.SMEM((STEPS, 128), i32),
            pltpu.SMEM((STEPS, 128), i32),
            pltpu.VMEM(queries.shape, bf16),
            pltpu.SMEM((32,), i32),
            pltpu.SMEM((32,), i32),
            pltpu.SMEM((8,), i32),
            pltpu.SMEM((64,), i32),
            pltpu.SMEM((64,), i32),
            pltpu.SMEM((64,), i32),
            pltpu.SemaphoreType.DMA((5,)),
        ],
        compiler_params=pltpu.CompilerParams(vmem_limit_bytes=VMEM),
        cost_estimate=pl.CostEstimate(flops=100_000_000, bytes_accessed=4_000_000, transcendentals=0),
        name="prep",
    )(tile_slot, tile_slot.reshape(8, 128), step_lengths.T, parents.T, queries)

    planes = lambda number, capacity: pl.pallas_call(
        functools.partial(plane_kernel, capacity),
        out_shape=jax.ShapeDtypeStruct((PROBLEMS * LIVE, columns), bf16),
        in_specs=[smem] + [hbm] * 5,
        out_specs=vmem,
        scratch_shapes=[pltpu.VMEM((PROBLEMS, HD, LANES), bf16)] * 8
        + [
            pltpu.VMEM((PROBLEMS, SPAN, LIVE), f32),
            pltpu.VMEM(step_kv.shape, bf16),
            pltpu.VMEM((2, 32, TILE, HD), bf16),
            pltpu.VMEM((3, capacity, 2, TILE, HD), bf16),
            pltpu.VMEM((3, capacity, 2, TILE, HD), bf16),
            pltpu.VMEM((64, 2, TILE, HD), bf16),
            pltpu.VMEM((Z, Y, HD, PART_A), bf16),
            pltpu.VMEM((Z, Y, HD, PART_B), bf16),
            pltpu.VMEM((8, PROBLEMS, LIVE, LANES), bf16),
            pltpu.VMEM((2, capacity, TILE, HD), bf16),
            pltpu.VMEM((9, HD, LANES), f32),
            pltpu.VMEM((9, 1, LANES), f32),
            pltpu.VMEM((9, 1, LANES), f32),
            pltpu.VMEM((PROBLEMS, HD, LANES), f32),
            pltpu.VMEM((PROBLEMS, 1, LANES), f32),
            pltpu.VMEM((PROBLEMS, 1, LANES), f32),
        ]
        + [
            pltpu.VMEM((4, PROBLEMS, HD, LANES), bf16),
            pltpu.VMEM((4, PROBLEMS, 1, 2 * LANES), f32),
        ]
        * 4
        + [
            pltpu.VMEM((PROBLEMS * LIVE, PART_B), f32),
            pltpu.SemaphoreType.DMA((8,)),
            pltpu.SemaphoreType.DMA((8, 6)),
            pltpu.SemaphoreType.DMA((8, 6)),
            pltpu.SemaphoreType.DMA((4, 2)),
            pltpu.SemaphoreType.DMA((4, 2)),
            pltpu.SemaphoreType.DMA((4, 2, 4, 2)),
            pltpu.SemaphoreType.DMA((4, 2, 4, 2)),
            pltpu.SemaphoreType.DMA((7, 4)),
            pltpu.SemaphoreType.DMA((7, 4)),
            pltpu.SemaphoreType.DMA((16, 2)),
            pltpu.SemaphoreType.DMA((16, 2)),
        ],
        compiler_params=pltpu.CompilerParams(
            collective_id=number, has_side_effects=True, vmem_limit_bytes=VMEM
        ),
        cost_estimate=pl.CostEstimate(
            flops=60_000_000_000, bytes_accessed=300_000_000, transcendentals=10_000_000
        ),
        name="planes",
    )
    compact = lax.switch(
        choice[0],
        [planes(number, capacity) for number, capacity in enumerate(CAPACITIES)],
        meta, qt, mask, step_kv, tile_kv.reshape(2, 32, TILE, HD), out_weight,
    )

    block = 512
    return pl.pallas_call(
        expand_kernel,
        out_shape=jax.ShapeDtypeStruct((PROBLEMS * SPAN, columns), bf16),
        grid=(columns // block,),
        in_specs=[
            pl.BlockSpec((PROBLEMS * LIVE, block), lambda i: (0, i)),
            pl.BlockSpec((PROBLEMS, SPAN, LIVE), lambda i: (0, 0, 0)),
        ],
        out_specs=pl.BlockSpec((PROBLEMS * SPAN, block), lambda i: (0, i)),
        compiler_params=pltpu.CompilerParams(vmem_limit_bytes=VMEM),
        cost_estimate=pl.CostEstimate(
            flops=200_000_000, bytes_accessed=3_000_000, transcendentals=0
        ),
        name="expand",
    )(compact, expand)


def solution(mesh):
    return jax.shard_map(
        per_device,
        mesh=mesh,
        in_specs=(
            P("dp", "tensor"),
            P(None, "dp", "tensor"),
            P(None, "dp", "tensor"),
            P(),
            P(),
            P(),
            P("dp", "tensor"),
        ),
        out_specs=P("dp", "tensor"),
        check_vma=False,
    )
```

```python
import functools
import math

import jax
import jax.numpy as jnp
from jax import lax
from jax.experimental import pallas as pl
from jax.experimental.pallas import tpu as pltpu
from jax.sharding import PartitionSpec as P

HD = 128
TILE = 256
STEPS = 8
STEP_LEN = 24
SPAN = STEPS * STEP_LEN
PROBLEMS = 4
GROUP = 4
LIVE = 128
LANES = GROUP * LIVE
Z = 8
Y = 4
X = 4
LOW = -1e30
SCALE = math.log2(math.e) / math.sqrt(HD)
MESH = pl.DeviceIdType.MESH
ORDER = (4, 3, 5, 2, 6, 1, 7, 0)
MIB = 1 << 20
VMEM = 60 * MIB
PART_A = 256
PART_B = 768
HALVES = ((2, 4), (0, 2))
AHEAD = 5
B2_TURN = 3

META_ORDER = 0
META_OWNER = 64
META_SAME = 128
META_LAST = 192
META_SOURCE = 256
CAPACITIES = (12, 13, 16)


class Pair:
    def __init__(self, copy, leaving, arriving):
        self.start = lambda: copy(leaving).start()
        self.wait_send = lambda: copy(leaving).wait_send()
        self.wait_recv = lambda: copy(arriving).wait_recv()


def dot(a, b, dims=((1,), (0,))):
    return lax.dot_general(a, b, (dims, ((), ())), preferred_element_type=jnp.float32)


def prep_kernel(
    slot_hbm, table_hbm, length_hbm, parent_hbm, query_hbm,
    qt_ref, mask_ref, expand_ref, meta_ref, choice_ref,
    slot_ref, table_ref, length_ref, parent_ref, query_ref,
    count, count_in, rank, given, taken, place_of, sems,
):
    loads = [
        pltpu.make_async_copy(source, target, sems.at[i])
        for i, (source, target) in enumerate(
            (
                (slot_hbm, slot_ref),
                (table_hbm, table_ref),
                (length_hbm, length_ref),
                (parent_hbm, parent_ref),
                (query_hbm, query_ref),
            )
        )
    ]
    for load in loads:
        load.start()
    dp = lax.axis_index("dp")
    z, y = dp // Y, dp % Y

    def clear(i, _):
        count[i] = 0
        count_in[i] = 0
        return 0

    lax.fori_loop(0, 32, clear, 0)

    def clear_slots(i, _):
        given[i] = -1
        taken[i] = -1
        meta_ref[META_ORDER + i] = 0
        meta_ref[META_OWNER + i] = 0
        meta_ref[META_SAME + i] = 0
        meta_ref[META_LAST + i] = 0
        meta_ref[META_SOURCE + i] = 0
        return 0

    lax.fori_loop(0, 64, clear_slots, 0, unroll=8)
    for i, rz in enumerate(ORDER):
        rank[rz] = i
    loads[0].wait()

    def place(t, _):
        d = slot_ref[dp * 32 + t] >> 2
        turn = rank[((d >> 2) - z) & 7]
        r = ((d & 3) - y) & 3
        j = count[r * 8 + turn]
        count[r * 8 + turn] = j + 1
        given[r * 16 + turn * 2 + j] = t
        return 0

    lax.fori_loop(0, 32, place, 0, unroll=4)

    def arrive(q, _):
        s = slot_ref[z * 128 + q]
        d = s >> 2

        @pl.when((d & 3) == y)
        def _():
            turn = rank[((d >> 2) - z) & 7]
            r = (y - (q >> 5)) & 3
            j = count_in[r * 8 + turn]
            count_in[r * 8 + turn] = j + 1
            taken[r * 16 + turn * 2 + j] = s & 3

        return 0

    lax.fori_loop(0, 128, arrive, 0, unroll=8)

    def close(i, carry):
        sent, got = carry
        sent, got = jnp.where(i % 16 == 0, 0, sent), jnp.where(i % 16 == 0, 0, got)
        base = (i // 16) * 16
        tile = given[i]
        give, take = tile >= 0, taken[i] >= 0

        @pl.when(give)
        def _():
            meta_ref[META_SOURCE + base + sent] = tile

        place_of[i] = base + got
        return sent + give.astype(jnp.int32), got + take.astype(jnp.int32)

    lax.fori_loop(0, 64, close, (0, 0), unroll=8)

    def arrange(i, n):
        turn, p = i // 4, i % 4
        n = jnp.where(p == 0, 0, n)

        def scan(s, carry):
            n, seen = carry
            index = (s // 2) * 16 + turn * 2 + s % 2
            match = taken[index] == p

            @pl.when(match)
            def _():
                meta_ref[META_ORDER + turn * 8 + n] = place_of[index]
                meta_ref[META_OWNER + turn * 8 + n] = p
                meta_ref[META_SAME + turn * 8 + n] = seen
                meta_ref[META_LAST + turn * 4 + p] = n + 1

            hit = match.astype(jnp.int32)
            return n + hit, jnp.maximum(seen, hit)

        n, _ = lax.fori_loop(0, 8, scan, (n, 0), unroll=True)
        return n

    lax.fori_loop(0, 32, arrange, 0)

    for load in loads[1:]:
        load.wait()

    table = table_ref[...]
    column = (table >> 2) & 3
    lane = lax.broadcasted_iota(jnp.int32, (8, 128), 1) // 32
    block = lax.broadcasted_iota(jnp.int32, (128, 128), 0) // 32
    same_block = block == lax.broadcasted_iota(jnp.int32, (128, 128), 1) // 32
    ones = jnp.where(same_block, 1.0, 0.0).astype(jnp.bfloat16)
    most = jnp.zeros((8, 128), jnp.float32)
    for v in range(Y):
        hit = jnp.where((column == v) & (lane != v), 1.0, 0.0).astype(jnp.bfloat16)
        most = jnp.maximum(most, dot(hit, ones))
    most = jnp.max(most)
    choice = jnp.int32(0)
    for capacity in CAPACITIES[:-1]:
        choice = choice + (most > capacity + 0.5).astype(jnp.int32)
    choice_ref[0] = choice

    row = lax.broadcasted_iota(jnp.int32, (SPAN, LIVE), 0)
    lane = lax.broadcasted_iota(jnp.int32, (SPAN, LIVE), 1)
    step_of = row // STEP_LEN
    position = row - step_of * STEP_LEN
    for p in range(PROBLEMS):
        problem = dp * PROBLEMS + p
        lengths = [length_ref[s, problem] for s in range(STEPS)]
        links = [parent_ref[s, problem] for s in range(STEPS)]
        starts, lines = [], []
        total = jnp.int32(0)
        for s in range(STEPS):
            starts.append(total)
            total = total + lengths[s]
            line = jnp.int32(1 << s)
            for b in range(s):
                line = line | jnp.where(links[s] == b, lines[b], 0)
            lines.append(line)
        row_start, row_length = jnp.zeros_like(row), jnp.zeros_like(row)
        row_bit = jnp.zeros_like(row)
        lane_step, lane_start, lane_line = jnp.zeros_like(row), jnp.zeros_like(row), jnp.zeros_like(row)
        for s in range(STEPS):
            here = step_of == s
            row_start = jnp.where(here, starts[s], row_start)
            row_length = jnp.where(here, lengths[s], row_length)
            row_bit = jnp.where(here, 1 << s, row_bit)
            passed = lane >= starts[s]
            lane_step = jnp.where(passed, s, lane_step)
            lane_start = jnp.where(passed, starts[s], lane_start)
            lane_line = jnp.where(passed, lines[s], lane_line)
        live = position < row_length
        picked = (lane == row_start + position) & live
        expand = jnp.where(picked, 1.0, 0.0).astype(jnp.bfloat16)
        expand_ref[p] = expand
        visible = (
            ((lane_line & row_bit) != 0)
            & live
            & ((step_of != lane_step) | (position <= lane - lane_start))
        )
        mask_ref[p] = jnp.where(visible, 1.0, 0.0)
        for h in range(GROUP):
            block = query_ref[p * SPAN : (p + 1) * SPAN, h * HD : (h + 1) * HD]
            qt_ref[p, :, h * LIVE : (h + 1) * LIVE] = dot(block, expand, ((0,), (0,))).astype(
                jnp.bfloat16
            )


def plane_kernel(
    capacity,
    meta_ref, qt_hbm, mask_hbm, step_hbm, tile_hbm, weight_hbm,
    out_ref,
    *scratch,
):
    qs = scratch[0:8]
    (
        mask_ref, step_ref, own_ref, send_ref, here_ref, pool_ref, weights_a, weights_b, heads,
        relay, state_o, state_m, state_l, step_o, step_m, step_l,
        up_in, up_in_s, up_out, up_out_s, down_in, down_in_s, down_out, down_out_s,
        total_b, own_sem, y_send, y_recv, q_send, q_recv, c_send, c_recv, x_send, x_recv, w_send, w_recv,
    ) = scratch[8:]
    chunks = (capacity + 1) // 2
    dp, tensor = lax.axis_index("dp"), lax.axis_index("tensor")
    z, y = dp // Y, dp % Y
    x, core = tensor // 2, tensor % 2
    y_up = (z * Y + (y + 1) % Y, tensor)
    y_down = (z * Y + (y + Y - 1) % Y, tensor)
    z_up = (((z + 1) % Z) * Y + y, tensor)
    z_down = (((z + Z - 1) % Z) * Y + y, tensor)
    x_up = (dp, ((x + 1) % X) * 2 + core)
    x_down = (dp, ((x + X - 1) % X) * 2 + core)
    mate = (dp, x * 2 + 1 - core)

    loads = [
        pltpu.make_async_copy(source, target, own_sem.at[i])
        for i, (source, target) in enumerate(
            (
                (qt_hbm, qs[0]),
                (tile_hbm, own_ref),
                (weight_hbm.at[:, pl.ds(0, PART_A)], weights_a.at[z, y]),
                (weight_hbm.at[:, pl.ds(PART_A, PART_B)], weights_b.at[z, y]),
                (step_hbm, step_ref),
                (mask_hbm, mask_ref),
            )
        )
    ]
    for load in loads:
        load.start()

    barrier = pltpu.get_barrier_semaphore()
    peers = (y_up, y_down, z_up, z_down, x_up, x_down, mate)
    for peer in peers:
        pl.semaphore_signal(barrier, inc=1, device_id=peer, device_id_type=MESH)
    pl.semaphore_wait(barrier, len(peers))

    def remote(src, dst, send_sem, recv_sem, peer):
        return pltpu.make_async_remote_copy(
            src_ref=src, dst_ref=dst, send_sem=send_sem, recv_sem=recv_sem,
            device_id=peer, device_id_type=MESH,
        )

    def q_copies(hop):
        up_from, up_to = (8 - hop) % 8, 7 - hop
        up_src, up_dst = qs[up_from], qs[up_to]
        down_src, down_dst = qs[hop], qs[hop + 1]
        if hop == 3:
            up_src, up_dst = up_src.at[pl.ds(0, 2)], up_dst.at[pl.ds(0, 2)]
            down_src, down_dst = down_src.at[pl.ds(2, 2)], down_dst.at[pl.ds(2, 2)]
        return (
            remote(up_src, up_dst, q_send.at[hop, 0], q_recv.at[hop, 0], z_up),
            remote(down_src, down_dst, q_send.at[hop, 1], q_recv.at[hop, 1], z_down),
        )

    def span(i):
        return pl.ds(2 * i, min(2, capacity - 2 * i))

    def direct(i):
        at = span(i)
        return (
            remote(send_ref.at[0, at], here_ref.at[0, at], y_send.at[i, 0], y_recv.at[i, 0], y_up),
            remote(send_ref.at[2, at], here_ref.at[2, at], y_send.at[i, 1], y_recv.at[i, 1], y_down),
        )

    def first_leg(i):
        at = span(i)
        return (
            remote(send_ref.at[1, at, 0], relay.at[0, at], y_send.at[i, 2], y_recv.at[i, 2], y_up),
            remote(send_ref.at[1, at, 1], relay.at[1, at], y_send.at[i, 3], y_recv.at[i, 3], y_down),
        )

    def second_leg(i):
        at = span(i)
        return (
            remote(relay.at[0, at], here_ref.at[1, at, 0], y_send.at[i, 4], y_recv.at[i, 4], y_up),
            remote(relay.at[1, at], here_ref.at[1, at, 1], y_send.at[i, 5], y_recv.at[i, 5], y_down),
        )

    def pack(i):
        def give(k, _):
            for r in range(1, Y):
                send_ref[r - 1, k] = own_ref[:, meta_ref[META_SOURCE + r * 16 + k]]
            return 0

        lax.fori_loop(2 * i, min(2 * i + 2, capacity), give, 0)

    def keep(k, _):
        pool_ref[k] = own_ref[:, meta_ref[META_SOURCE + k]]
        return 0

    def join(i):
        arrived(direct(i))
        arrived(second_leg(i))
        for r in range(1, Y):
            for k in range(2 * i, min(2 * i + 2, capacity)):
                pool_ref[r * 16 + k] = here_ref[r - 1, k]

    def along_z(view, low, high, k, hop):
        up_block, down_block = view((z + Z - hop) % Z), view((z + hop) % Z)
        up_next, down_next = view((z + Z - hop - 1) % Z), view((z + hop + 1) % Z)
        if hop == 3:
            up_block, up_next = up_block.at[low], up_next.at[low]
            down_block, down_next = down_block.at[high], down_next.at[high]
        return ring_pair(up_block, up_next, z_up, down_block, down_next, z_down, k + hop)

    def along_y(view, low, high, k, hop):
        up_block, down_block = view((y + Y - hop) % Y), view((y + hop) % Y)
        up_next, down_next = view((y + Y - hop - 1) % Y), view((y + hop + 1) % Y)
        if hop == 1:
            up_block, up_next = up_block.at[low], up_next.at[low]
            down_block, down_next = down_block.at[high], down_next.at[high]
        return ring_pair(up_block, up_next, y_up, down_block, down_next, y_down, k + hop)

    def ring_pair(up_block, up_next, up_peer, down_block, down_next, down_peer, k):
        def side(i, peer):
            return lambda block: remote(block, block, w_send.at[k, i], w_recv.at[k, i], peer)

        return (
            Pair(side(0, up_peer), up_block, up_next),
            Pair(side(1, down_peer), down_block, down_next),
        )

    first_rows, last_rows = pl.ds(0, HD // 2), pl.ds(HD // 2, HD // 2)

    def a1(hop):
        return along_y(lambda k: weights_a.at[z, k], first_rows, last_rows, 0, hop)

    def a2(hop):
        return along_z(lambda k: weights_a.at[k], pl.ds(0, 2), pl.ds(2, 2), 2, hop)

    def b1(hop):
        return along_z(lambda k: weights_b.at[k, y], first_rows, last_rows, 6, hop)

    def planes_pair(k, distance):
        return weights_b.at[pl.ds(2 * k, 2), (y + distance) % Y]

    def b2_near(k):
        other = (k + 2) % 4
        return ring_pair(
            planes_pair(k, 0), planes_pair(k, 3), y_up,
            planes_pair(other, 0), planes_pair(other, 1), y_down, 10 + k,
        )

    def b2_far(k):
        return ring_pair(
            planes_pair(k, 3), planes_pair(k, 2), y_up,
            planes_pair(k + 2, 1), planes_pair(k + 2, 2), y_down, 14 + k,
        )

    def start(copies):
        for copy in copies:
            copy.start()

    def arrived(copies):
        for copy in copies:
            copy.wait_recv()

    def pass_on(i):
        arrived(first_leg(i))
        start(second_leg(i))

    loads[0].wait()
    start(q_copies(0))
    loads[2].wait()
    loads[3].wait()
    loads[1].wait()
    for i in range(AHEAD):
        pack(i)
        start(first_leg(i))
        start(direct(i))
        if i == 0:
            start(a1(0))
            start(b1(0))
    lax.fori_loop(0, 16, keep, 0)

    state_o[0] = jnp.zeros((HD, LANES), jnp.float32)
    state_m[0] = jnp.full((1, LANES), LOW, jnp.float32)
    state_l[0] = jnp.zeros((1, LANES), jnp.float32)

    def soften(scores, m_before):
        m = jnp.maximum(m_before, jnp.max(scores, axis=0, keepdims=True))
        expo = jnp.exp2(scores - m)
        return m, jnp.sum(expo, axis=0, keepdims=True), expo.astype(jnp.bfloat16)

    def attend_steps(p, _):
        rows = pl.ds(pl.multiple_of(p * SPAN, SPAN), SPAN)
        mask = mask_ref[p]
        mask = jnp.concatenate([mask] * GROUP, axis=1)
        scores = dot(step_ref[0, rows, :], qs[0][p]) * SCALE
        scores = jnp.where(mask > 0.5, scores, LOW)
        m, l, weights = soften(scores, jnp.full((1, LANES), LOW, jnp.float32))
        step_o[p] = dot(step_ref[1, rows, :], weights, ((0,), (0,)))
        step_m[p] = m
        step_l[p] = l
        return 0

    def attend_tiles(turn):
        queries = qs[ORDER[turn]]

        def one(s, _):
            slot = meta_ref[META_ORDER + turn * 8 + s]
            owner = meta_ref[META_OWNER + turn * 8 + s]
            same = meta_ref[META_SAME + turn * 8 + s]
            scores = dot(pool_ref[slot, 0], queries[owner]) * SCALE
            m_before = jnp.where(same > 0, state_m[s], LOW)
            m, l, weights = soften(scores, m_before)
            alpha = jnp.exp2(m_before - m)
            state_o[s + 1] = state_o[s] * alpha + dot(pool_ref[slot, 1], weights, ((0,), (0,)))
            state_m[s + 1] = m
            state_l[s + 1] = state_l[s] * alpha + l
            return 0

        lax.fori_loop(0, 8, one, 0, unroll=2)

    def sums(hop, p, side):
        out, out_s, inn, inn_s, peer = (
            (up_out, up_out_s, up_in, up_in_s, z_up),
            (down_out, down_out_s, down_in, down_in_s, z_down),
        )[side]
        return (
            remote(out.at[hop, p], inn.at[hop, p], c_send.at[hop, side, p, 0], c_recv.at[hop, side, p, 0], peer),
            remote(out_s.at[hop, p], inn_s.at[hop, p], c_send.at[hop, side, p, 1], c_recv.at[hop, side, p, 1], peer),
        )

    def pass_sums(hop, turn, side):
        out, out_s, inn, inn_s = (
            (up_out, up_out_s, up_in, up_in_s),
            (down_out, down_out_s, down_in, down_in_s),
        )[side]

        def alone(p, _):
            last = meta_ref[META_LAST + turn * 4 + p]
            out[hop, p] = state_o[last].astype(jnp.bfloat16)
            out_s[hop, p, :, 0:LANES] = state_m[last]
            out_s[hop, p, :, LANES:] = state_l[last]
            start(sums(hop, p, side))
            return 0

        def merged(p, _):
            last = meta_ref[META_LAST + turn * 4 + p]
            arrived(sums(hop - 1, p, side))
            m_a, m_b = state_m[last], inn_s[hop - 1, p, :, 0:LANES]
            m = jnp.maximum(m_a, m_b)
            a, b = jnp.exp2(m_a - m), jnp.exp2(m_b - m)
            out[hop, p] = (state_o[last] * a + inn[hop - 1, p].astype(jnp.float32) * b).astype(
                jnp.bfloat16
            )
            out_s[hop, p, :, 0:LANES] = m
            out_s[hop, p, :, LANES:] = state_l[last] * a + inn_s[hop - 1, p, :, LANES:] * b
            start(sums(hop, p, side))
            return 0

        half = HALVES[side]
        if hop == 0:
            lax.fori_loop(*half, alone, 0)
        elif hop == 1 and side == 0:
            lax.fori_loop(0, 2, alone, 0)
            lax.fori_loop(2, 4, merged, 0)
        elif hop == 1:
            lax.fori_loop(0, 2, merged, 0)
            lax.fori_loop(2, 4, alone, 0)
        else:
            lax.fori_loop(0, 4, merged, 0)

    for hop in range(3):
        arrived(q_copies(hop))
        start(q_copies(hop + 1))
        pass_on(hop)
        arrived(b1(hop))
        start(b1(hop + 1))
        if hop == 0:
            arrived(a1(0))
            start(a1(1))
    for i in range(3, AHEAD):
        pass_on(i)
    loads[4].wait()
    loads[5].wait()
    lax.fori_loop(0, PROBLEMS, attend_steps, 0)
    arrived(a1(1))

    legs = {
        0: [(b1, 3, None, 0)],
        6: [(None, 0, a2, 0)],
    }
    for i in range(8):
        rz = ORDER[i]
        if i < chunks:
            join(i)
        ahead = i + AHEAD
        if ahead < chunks:
            pack(ahead)
            start(first_leg(ahead))
            start(direct(ahead))
        if AHEAD <= ahead - 1 < chunks:
            pass_on(ahead - 1)
        if i == 0:
            arrived(q_copies(3))
        if i == B2_TURN:
            for k in range(4):
                start(b2_near(k))
        attend_tiles(i)
        if rz == 4:
            pass_sums(0, i, 0)
            pass_sums(0, i, 1)
        elif rz in (3, 2, 1):
            pass_sums(4 - rz, i, 0)
        elif rz in (5, 6, 7):
            pass_sums(rz - 4, i, 1)
        for before, hop, after, next_hop in legs.get(i, ()):
            if before is not None:
                arrived(before(hop))
            if after is not None:
                start(after(next_hop))
        if i == 6:
            arrived(b2_near(0))
            start(b2_far(0))
    mine = tensor

    def finish(p):
        arrived(sums(3, p, 0))
        arrived(sums(3, p, 1))
        last = meta_ref[META_LAST + 28 + p]
        terms = (
            (state_o[last], state_m[last], state_l[last]),
            (step_o[p], step_m[p], step_l[p]),
            (up_in[3, p].astype(jnp.float32), up_in_s[3, p, :, 0:LANES], up_in_s[3, p, :, LANES:]),
            (down_in[3, p].astype(jnp.float32), down_in_s[3, p, :, 0:LANES], down_in_s[3, p, :, LANES:]),
        )
        m = functools.reduce(jnp.maximum, [t[1] for t in terms])
        factors = [jnp.exp2(t[1] - m) for t in terms]
        total = sum(t[2] * f for t, f in zip(terms, factors))
        result = sum(t[0] * f for t, f in zip(terms, factors)) / total
        for h in range(GROUP):
            block = result[:, h * LIVE : (h + 1) * LIVE]
            heads[mine, p, :, h * HD : (h + 1) * HD] = block.T.astype(jnp.bfloat16)

    left, right, far = (x + X - 1) % X, (x + 1) % X, (x + 2) % X

    def to(k, p, owner, peer):
        view = heads.at[owner, p]
        return remote(view, view, x_send.at[k, p], x_recv.at[k, p], peer)

    def own_heads(p):
        return to(0, p, mine, x_up), to(1, p, mine, x_down), to(2, p, mine, mate)

    def next_heads(p):
        onward = to(3, p, left * 2 + core, x_up) if p < 2 else to(3, p, right * 2 + core, x_down)
        return onward, to(4, p, left * 2 + core, mate), to(5, p, right * 2 + core, mate)

    def near_heads(p):
        return to(0, p, left * 2 + core, x_up), to(1, p, right * 2 + core, x_down)

    def far_heads(p):
        return (to(3, p, far * 2 + core, x_up if p < 2 else x_down),)

    def last_heads(p):
        return (to(6, p, far * 2 + core, mate),)

    def mate_heads(p):
        other = 1 - core
        return (
            to(2, p, x * 2 + other, mate),
            to(4, p, left * 2 + other, mate),
            to(5, p, right * 2 + other, mate),
            to(6, p, far * 2 + other, mate),
        )

    for p in range(PROBLEMS):
        finish(p)
        start(own_heads(p))
        if p > 0:
            arrived(near_heads(p - 1))
            start(next_heads(p - 1))
        if p == 2:
            arrived(a2(0))
            start(a2(1))
            arrived(b2_near(1))
            start(b2_far(1))
    arrived(near_heads(3))
    start(next_heads(3))
    arrived(a2(1))
    start(a2(2))
    for p in range(PROBLEMS):
        arrived(far_heads(p))
        start(last_heads(p))
    arrived(a2(2))
    start(a2(3))
    for p in range(PROBLEMS):
        arrived(mate_heads(p))

    def product(weights, t, columns):
        block = weights[t, :, :, columns].reshape(LANES, 256)
        return dot(heads[t].reshape(PROBLEMS * LIVE, LANES), block)

    def part_b(planes, more):
        def block(c, _):
            columns = pl.ds(pl.multiple_of(c * 256, 256), 256)
            total = sum(product(weights_b, t, columns) for t in planes)
            into = pl.ds(pl.multiple_of(PART_A + c * 256, 256), 256)
            if more:
                total_b[:, columns] = total
            else:
                out_ref[:, into] = (total_b[:, columns] + total).astype(jnp.bfloat16)
            return 0

        lax.fori_loop(0, PART_B // 256, block, 0)

    for k in range(2, 4):
        arrived(b2_near(k))
    arrived(b2_far(0))
    part_b((0, 1, 4, 5), True)
    arrived(a2(3))
    total_a = sum(product(weights_a, t, pl.ds(0, PART_A)) for t in range(8))
    out_ref[:, 0:PART_A] = total_a.astype(jnp.bfloat16)
    arrived(b2_far(1))
    part_b((2, 3, 6, 7), False)

    for p in range(PROBLEMS):
        for copy in own_heads(p) + next_heads(p) + last_heads(p):
            copy.wait_send()
    for hop in range(4):
        for copy in q_copies(hop) + a2(hop) + b1(hop):
            copy.wait_send()
        for side in range(2):
            for p in range(*HALVES[side]) if hop == 0 else range(PROBLEMS):
                for copy in sums(hop, p, side):
                    copy.wait_send()
    for hop in range(2):
        for copy in a1(hop) + b2_far(hop):
            copy.wait_send()
    for k in range(4):
        for copy in b2_near(k):
            copy.wait_send()
    for i in range(chunks):
        for copy in direct(i) + first_leg(i) + second_leg(i):
            copy.wait_send()


def expand_kernel(compact_ref, expand_ref, out_ref):
    for p in range(PROBLEMS):
        out_ref[p * SPAN : (p + 1) * SPAN, :] = dot(
            expand_ref[p], compact_ref[p * LIVE : (p + 1) * LIVE, :]
        ).astype(jnp.bfloat16)


def per_device(queries, step_kv, tile_kv, tile_slot, step_lengths, parents, out_weight):
    bf16, f32, i32 = jnp.bfloat16, jnp.float32, jnp.int32
    smem = pl.BlockSpec(memory_space=pltpu.SMEM)
    vmem = pl.BlockSpec(memory_space=pltpu.VMEM)
    hbm = pl.BlockSpec(memory_space=pl.ANY)
    columns = out_weight.shape[1]

    qt, mask, expand, meta, choice = pl.pallas_call(
        prep_kernel,
        out_shape=(
            jax.ShapeDtypeStruct((PROBLEMS, HD, LANES), bf16),
            jax.ShapeDtypeStruct((PROBLEMS, SPAN, LIVE), f32),
            jax.ShapeDtypeStruct((PROBLEMS, SPAN, LIVE), bf16),
            jax.ShapeDtypeStruct((512,), i32),
            jax.ShapeDtypeStruct((1,), i32),
        ),
        in_specs=[hbm] * 5,
        out_specs=(vmem, vmem, vmem, smem, smem),
        scratch_shapes=[
            pltpu.SMEM((1024,), i32),
            pltpu.VMEM((8, 128), i32),
            pltpu.SMEM((STEPS, 128), i32),
            pltpu.SMEM((STEPS, 128), i32),
            pltpu.VMEM(queries.shape, bf16),
            pltpu.SMEM((32,), i32),
            pltpu.SMEM((32,), i32),
            pltpu.SMEM((8,), i32),
            pltpu.SMEM((64,), i32),
            pltpu.SMEM((64,), i32),
            pltpu.SMEM((64,), i32),
            pltpu.SemaphoreType.DMA((5,)),
        ],
        compiler_params=pltpu.CompilerParams(vmem_limit_bytes=VMEM),
        cost_estimate=pl.CostEstimate(flops=100_000_000, bytes_accessed=4_000_000, transcendentals=0),
        name="prep",
    )(tile_slot, tile_slot.reshape(8, 128), step_lengths.T, parents.T, queries)

    planes = lambda number, capacity: pl.pallas_call(
        functools.partial(plane_kernel, capacity),
        out_shape=jax.ShapeDtypeStruct((PROBLEMS * LIVE, columns), bf16),
        in_specs=[smem] + [hbm] * 5,
        out_specs=vmem,
        scratch_shapes=[pltpu.VMEM((PROBLEMS, HD, LANES), bf16)] * 8
        + [
            pltpu.VMEM((PROBLEMS, SPAN, LIVE), f32),
            pltpu.VMEM(step_kv.shape, bf16),
            pltpu.VMEM((2, 32, TILE, HD), bf16),
            pltpu.VMEM((3, capacity, 2, TILE, HD), bf16),
            pltpu.VMEM((3, capacity, 2, TILE, HD), bf16),
            pltpu.VMEM((64, 2, TILE, HD), bf16),
            pltpu.VMEM((Z, Y, HD, PART_A), bf16),
            pltpu.VMEM((Z, Y, HD, PART_B), bf16),
            pltpu.VMEM((8, PROBLEMS, LIVE, LANES), bf16),
            pltpu.VMEM((2, capacity, TILE, HD), bf16),
            pltpu.VMEM((9, HD, LANES), f32),
            pltpu.VMEM((9, 1, LANES), f32),
            pltpu.VMEM((9, 1, LANES), f32),
            pltpu.VMEM((PROBLEMS, HD, LANES), f32),
            pltpu.VMEM((PROBLEMS, 1, LANES), f32),
            pltpu.VMEM((PROBLEMS, 1, LANES), f32),
        ]
        + [
            pltpu.VMEM((4, PROBLEMS, HD, LANES), bf16),
            pltpu.VMEM((4, PROBLEMS, 1, 2 * LANES), f32),
        ]
        * 4
        + [
            pltpu.VMEM((PROBLEMS * LIVE, PART_B), f32),
            pltpu.SemaphoreType.DMA((8,)),
            pltpu.SemaphoreType.DMA((8, 6)),
            pltpu.SemaphoreType.DMA((8, 6)),
            pltpu.SemaphoreType.DMA((4, 2)),
            pltpu.SemaphoreType.DMA((4, 2)),
            pltpu.SemaphoreType.DMA((4, 2, 4, 2)),
            pltpu.SemaphoreType.DMA((4, 2, 4, 2)),
            pltpu.SemaphoreType.DMA((7, 4)),
            pltpu.SemaphoreType.DMA((7, 4)),
            pltpu.SemaphoreType.DMA((16, 2)),
            pltpu.SemaphoreType.DMA((16, 2)),
        ],
        compiler_params=pltpu.CompilerParams(
            collective_id=number, has_side_effects=True, vmem_limit_bytes=VMEM
        ),
        cost_estimate=pl.CostEstimate(
            flops=60_000_000_000, bytes_accessed=300_000_000, transcendentals=10_000_000
        ),
        name="planes",
    )
    compact = lax.switch(
        choice[0],
        [planes(number, capacity) for number, capacity in enumerate(CAPACITIES)],
        meta, qt, mask, step_kv, tile_kv.reshape(2, 32, TILE, HD), out_weight,
    )

    block = 512
    return pl.pallas_call(
        expand_kernel,
        out_shape=jax.ShapeDtypeStruct((PROBLEMS * SPAN, columns), bf16),
        grid=(columns // block,),
        in_specs=[
            pl.BlockSpec((PROBLEMS * LIVE, block), lambda i: (0, i)),
            pl.BlockSpec((PROBLEMS, SPAN, LIVE), lambda i: (0, 0, 0)),
        ],
        out_specs=pl.BlockSpec((PROBLEMS * SPAN, block), lambda i: (0, i)),
        compiler_params=pltpu.CompilerParams(vmem_limit_bytes=VMEM),
        cost_estimate=pl.CostEstimate(
            flops=200_000_000, bytes_accessed=3_000_000, transcendentals=0
        ),
        name="expand",
    )(compact, expand)


def solution(mesh):
    return jax.shard_map(
        per_device,
        mesh=mesh,
        in_specs=(
            P("dp", "tensor"),
            P(None, "dp", "tensor"),
            P(None, "dp", "tensor"),
            P(),
            P(),
            P(),
            P("dp", "tensor"),
        ),
        out_specs=P("dp", "tensor"),
        check_vma=False,
    )
```
